256 devices in a mesh: fsdp: 8 (over x, core), ep: 32 (over z, y).
Axes of the slice: x: 4, y: 4, z: 8, core: 2. Of those that a mesh axis runs over, the one named last changes fastest.
Arguments:
- out_grad: bfloat16 [4096, 7168], P('ep', 'fsdp'), may hold values from -1.5 to 1.5
- router_input: bfloat16 [4096, 7168], P('ep', 'fsdp'), may hold values from -6 to 6
- router_weight: float32 [7168, 32], P('fsdp'), may hold values from -0.0625 to 0.0625
- routes: int32 [4096, 8], P('ep'), may hold values from 0 to 31, all different within a row; in each aligned block of 128 rows (0 to 127, 128 to 255, ...) at most 36 rows name the same one
- balance_grad: float32 [4096, 32], P('ep'), may hold values from -6 to 6
- saved_hidden: bfloat16 [32, 32, 36, 2048], P('ep', None, None, 'fsdp'), may hold values from -6 to 6
- expert_down: bfloat16 [32, 2048, 7168], P('ep', None, 'fsdp'), may hold values from -0.125 to 0.125
- attention_grads: bfloat16 [32, 4, 288, 7168], P('ep', None, None, 'fsdp'), may hold values from -6 to 6
Outputs:
- grad_hidden: bfloat16 [32, 32, 36, 2048], P('ep', None, None, 'fsdp')
- grad_down: bfloat16 [32, 2048, 7168], P('ep', None, 'fsdp')
- router_grad: float32 [7168, 32], P('fsdp')
- token_grad: bfloat16 [4096, 7168], P('ep', 'fsdp')
- muon_update: bfloat16 [4, 288, 7168], P(None, None, 'fsdp')
The draws below stay inside these ranges and needn't reach their ends.
Inputs may be any that keep to these rules, and one draw needn't show every extreme that they name: `routes`: each expert is named by at most 36 of the rows of one device's block of 128 tokens, and by exactly 36 in some block; a row names 8 different experts.
All inputs are finite; a program needn't handle non-finite values.
Results may differ from the reference program's by a relative error of at most 0.029.
Values may be sent and summed in bfloat16 or wider, within the bound.
No kernel may reach another device: no remote copies, remote signals or barrier semaphores. Data moves between devices by JAX's collectives and lax.ppermute only.
A program may use at most 128 MiB of HBM per device.

```python
import math
import jax
import jax.numpy as jnp
import numpy as np
from jax import lax

D = 7168
FE = 2048
LATENT = 288
TOPK = 8
NS_ITERS = 2
TOK_DEV = 128
EXPERTS = 32
TOKENS = 4096
CAP = 36
MATS = 4
N_EP = 32


def level_of(key, extent, shards, smallest, largest):
    def one(axis_at, parts):
        heights = jax.random.uniform(jax.random.fold_in(jax.random.fold_in(key, 6), axis_at), (parts,), jnp.float32, smallest / len(shards), largest / len(shards))
        return jnp.repeat(jnp.exp(heights), extent[axis_at] // parts).reshape((-1,) + (1,) * (len(extent) - axis_at - 1))

    level = one(*shards[0])
    for cut in shards[1:]:
        level = level * one(*cut)
    return level


def routed_block(stream_key, own, number, rows, amount, top, limit, lean):
    sequence = jax.random.permutation(stream_key, amount)
    crowded, usual = shares(amount, rows * top, limit, lean, True), shares(amount, rows * top, limit, lean, False)
    places = jnp.arange(amount)

    def named(sizes, turn):
        used = int((sizes > 0).sum())
        fixed = max(1, used // 4)
        shifted = fixed + (places - fixed + turn * (used - fixed)) % max(1, amount - fixed)
        return jnp.zeros((amount,), jnp.int32).at[sequence[jnp.where(places < fixed, places, shifted)]].set(jnp.asarray(sizes, jnp.int32))

    sizes = jnp.where(number % 4 == 0, named(crowded, number // 4), named(usual, number - number // 4 - 1))
    mixed = jax.random.permutation(jax.random.fold_in(own, 3), amount)
    donor, receiver = mixed[0:amount // 2 * 2:2], mixed[1:amount // 2 * 2:2]
    slack = jnp.minimum(sizes[donor] - 1, limit - sizes[receiver]) // 2
    slack = jnp.where((donor == sequence[0]) | (receiver == sequence[0]) | (sizes[receiver] == 0), 0, jnp.maximum(slack, 0))
    shifted = jax.random.randint(jax.random.fold_in(own, 4), (amount // 2,), 0, 1 << 20) % (slack + 1)
    sizes = sizes.at[donor].add(-shifted).at[receiver].add(shifted)
    members = jnp.searchsorted(jnp.cumsum(sizes), jnp.arange(rows * top), side="right").astype(jnp.int32)
    table = members.reshape(top, rows).T
    table = table[jax.random.permutation(jax.random.fold_in(own, 1), rows)]
    turn = jax.random.randint(jax.random.fold_in(own, 2), (rows, 1), 0, top)
    return jnp.take_along_axis(table, (jnp.arange(top)[None, :] + turn) % top, axis=1)


def shares(number_of, total, reach, lean, full):
    loads = [(1 << 20) // math.isqrt(grade ** lean) + 1 for grade in range(1, number_of + 1)]
    largest = reach if full else min(reach, max(-(-total // number_of), total * loads[0] // sum(loads)))
    least = 1 if total - largest >= number_of - 1 else 0
    counts, spare = [largest] + [least] * (number_of - 1), total - largest - least * (number_of - 1)
    while spare > 0:
        candidates = [i for i in range(1, number_of) if counts[i] < largest] or [i for i in range(1, number_of) if counts[i] < reach]
        mass, budget = sum([loads[i] for i in candidates]), spare
        for i in candidates:
            extra = min(reach - counts[i], max(1, budget * loads[i] // mass), spare)
            counts[i] = counts[i] + extra
            spare = spare - extra
    return np.array(counts)


def centred(key, extent, scale, reach, split=(), held_as=jnp.bfloat16):
    values = scale * jax.random.normal(key, extent, jnp.float32)
    if split:
        values = values * level_of(key, extent, split, -0.22, 0.18)
    return jnp.clip(values, -reach, reach).astype(held_as)


def setup_inputs(seed: int = 0) -> dict:
    key_of = jax.random.split(jax.random.key(seed), 9)
    out_grad = centred(key_of[0], (TOKENS, D), 0.25, 1.5, ((0, 32), (1, 8)))
    router_input = centred(key_of[1], (TOKENS, D), 1.0, 6.0, ((0, 32), (1, 8)))
    router_weight = centred(key_of[2], (D, EXPERTS), D ** -0.5, 0.0625, ((0, 8),), jnp.float32)
    routes_keys = jax.random.split(jax.random.fold_in(key_of[3], 1), TOKENS // TOK_DEV)
    routes_turns = jax.random.permutation(jax.random.fold_in(key_of[3], 3), TOKENS // TOK_DEV)
    routes = jax.vmap(lambda own, number: routed_block(jax.random.fold_in(key_of[3], 2), own, number, TOK_DEV, EXPERTS, TOPK, CAP, 2))(routes_keys, routes_turns).reshape((TOKENS, TOPK))
    balance_grad = centred(key_of[4], (TOKENS, EXPERTS), 1.0, 6.0, ((0, 32),), jnp.float32)
    saved_hidden = centred(key_of[5], (EXPERTS, N_EP, CAP, FE), 1.0, 6.0, ((0, 32), (3, 8)))
    expert_down = centred(key_of[6], (EXPERTS, FE, D), FE ** -0.5, 0.125, ((0, 32), (2, 8)))
    attention_grads = centred(key_of[7], (N_EP, MATS, LATENT, D), 1.0, 6.0, ((0, 32), (3, 8)))
    return dict(out_grad=out_grad, router_input=router_input, router_weight=router_weight, routes=routes, balance_grad=balance_grad, saved_hidden=saved_hidden, expert_down=expert_down, attention_grads=attention_grads)


ROUTE_SCALE = 2.827
NORM_EPS = 1e-07
COEF_A = 3.4445
COEF_B = -4.775
COEF_C = 2.0315

def slot_tables(routes_block, experts, capacity):
    expert_ids = jnp.arange(experts, dtype=jnp.int32)
    chosen = jnp.any(routes_block[:, :, None] == expert_ids[None, None, :], axis=1)
    counted = jnp.cumsum(chosen.astype(jnp.int32), axis=0) - 1
    position = jnp.where(chosen, counted, -1)
    slot_ids = jnp.arange(capacity, dtype=jnp.int32)
    matches = position.T[:, None, :] == slot_ids[None, :, None]
    token_ids = jnp.arange(routes_block.shape[0], dtype=jnp.int32)
    source = lax.optimization_barrier(jnp.sum(jnp.where(matches, token_ids[None, None, :], 0), axis=2)).astype(jnp.int32)
    filled = jnp.any(matches, axis=2)
    return (chosen, matches, source, filled)

def orthogonalize(initial):
    current = initial
    for turn_index in range(NS_ITERS):
        values = current.astype(jnp.float32)
        gram_matrix = jnp.einsum('mrd,msd->mrs', values, values, precision=lax.Precision.HIGHEST).astype(jnp.bfloat16)
        gram_values = gram_matrix.astype(jnp.float32)
        square = jnp.einsum('mrs,mst->mrt', gram_values, gram_values, precision=lax.Precision.HIGHEST)
        blended = (COEF_B * gram_values + COEF_C * square).astype(jnp.bfloat16)
        product = jnp.einsum('mrs,msd->mrd', blended.astype(jnp.float32), values, precision=lax.Precision.HIGHEST)
        current = (COEF_A * values + product).astype(jnp.bfloat16)
    factor = 0.2 * jnp.sqrt(jnp.float32(max(LATENT, D)))
    return (factor * current.astype(jnp.float32)).astype(jnp.bfloat16)

def reference(out_grad, router_input, router_weight, routes, balance_grad, saved_hidden, expert_down, attention_grads):
    logits = jnp.dot(router_input.astype(jnp.float32), router_weight, precision=lax.Precision.HIGHEST)
    scores = jax.nn.sigmoid(logits)
    routes_blocks = routes.reshape(N_EP, TOK_DEV, TOPK)
    chosen, matches, source, filled = jax.vmap(lambda block: slot_tables(block, EXPERTS, CAP))(routes_blocks)
    selected = chosen.reshape(TOKENS, EXPERTS).astype(jnp.float32)
    score_total = lax.optimization_barrier(jnp.sum(selected * scores, axis=1, keepdims=True))
    gate_values = (selected * ROUTE_SCALE * scores / score_total).astype(jnp.bfloat16)
    gate_blocks = jnp.swapaxes(gate_values.reshape(N_EP, TOK_DEV, EXPERTS), 1, 2).astype(jnp.float32)
    slot_gates = lax.optimization_barrier(jnp.sum(jnp.where(matches, gate_blocks[:, :, None, :], 0.0), axis=3)).astype(jnp.bfloat16)
    grad_blocks = out_grad.reshape(N_EP, TOK_DEV, D)

    def expert_step(index):
        picked = jnp.take_along_axis(grad_blocks, source[:, index, :, None], axis=1)
        picked = jnp.where(filled[:, index][:, :, None], picked, jnp.zeros((), jnp.bfloat16))
        rows_flat = picked.reshape(N_EP * CAP, D)
        gate_flat = slot_gates[:, index].reshape(N_EP * CAP, 1).astype(jnp.float32)
        hidden_flat = saved_hidden[index].reshape(N_EP * CAP, FE)
        upstream = lax.dot_general(rows_flat, expert_down[index], (((1,), (1,)), ((), ())), preferred_element_type=jnp.float32)
        hidden_grad = (gate_flat * upstream).astype(jnp.bfloat16).reshape(N_EP, CAP, FE)
        scaled = (gate_flat * rows_flat.astype(jnp.float32)).astype(jnp.bfloat16)
        down_grad = lax.dot_general(hidden_flat, scaled, (((0,), (0,)), ((), ())), preferred_element_type=jnp.float32).astype(jnp.bfloat16)
        gate_grad = lax.optimization_barrier(jnp.sum(hidden_flat.astype(jnp.float32) * upstream, axis=1)).reshape(N_EP, CAP)
        return (hidden_grad, down_grad, gate_grad)
    grad_hidden, grad_down, gate_grads = lax.map(expert_step, jnp.arange(EXPERTS, dtype=jnp.int32))
    per_block = jnp.swapaxes(gate_grads, 0, 1)
    gate_back = lax.optimization_barrier(jnp.sum(jnp.where(matches, per_block[:, :, :, None], 0.0), axis=2))
    gate_back = jnp.swapaxes(gate_back, 1, 2).reshape(TOKENS, EXPERTS)
    weighted = lax.optimization_barrier(jnp.sum(selected * gate_back * scores, axis=1, keepdims=True)) / score_total
    score_grad = balance_grad + selected * (ROUTE_SCALE / score_total) * (gate_back - weighted)
    logit_grad = score_grad * scores * (1.0 - scores)
    router_grad = jnp.dot(router_input.astype(jnp.float32).T, logit_grad, precision=lax.Precision.HIGHEST)
    token_grad = jnp.dot(logit_grad, router_weight.T, precision=lax.Precision.HIGHEST).astype(jnp.bfloat16)

    def add_partial(carry, piece):
        return (carry + piece.astype(jnp.float32), None)
    summed, unused = lax.scan(add_partial, jnp.zeros((MATS, LATENT, D), jnp.float32), attention_grads)
    squares = lax.optimization_barrier(jnp.sum(summed * summed, axis=(1, 2)))
    initial = (summed / (jnp.sqrt(squares)[:, None, None] + NORM_EPS)).astype(jnp.bfloat16)
    muon_update = orthogonalize(initial)
    return (grad_hidden, grad_down, router_grad, token_grad, muon_update)
```

```python
import jax
import jax.numpy as jnp
from jax import lax
from jax.experimental import pallas as pl
from jax.experimental.pallas import tpu as pltpu
from jax.sharding import Mesh, PartitionSpec as P

D = 7168
LATENT = 288
ROUTE_SCALE = 2.827
NORM_EPS = 1e-07
COEF_A = 3.4445
COEF_B = -4.775
COEF_C = 2.0315
CAP = 36
SLOTS = 40
EXPERTS = 32
TOK = 128

FS = ("x", "c")
EP = ("z", "y")
f32 = jnp.float32
bf16 = jnp.bfloat16
VMEM_LIMIT = 48 * 1024 * 1024


def pack_kernel(routes_ref, tokens_ref, out_ref, pos_ref):
    expert_ids = lax.broadcasted_iota(jnp.int32, (EXPERTS, TOK), 0)
    chosen = jnp.zeros((EXPERTS, TOK), f32)
    for k in range(routes_ref.shape[0]):
        chosen = chosen + jnp.where(routes_ref[k : k + 1, :] == expert_ids, 1.0, 0.0)
    before = lax.broadcasted_iota(jnp.int32, (TOK, TOK), 0)
    after = lax.broadcasted_iota(jnp.int32, (TOK, TOK), 1)
    upper = jnp.where(before <= after, 1.0, 0.0).astype(bf16)
    counted = jnp.dot(chosen.astype(bf16), upper, preferred_element_type=f32)
    position = jnp.where(chosen > 0.0, counted - 1.0, -1.0)
    pos_ref[...] = position
    slot_ids = lax.broadcasted_iota(jnp.int32, (SLOTS, TOK), 0).astype(f32)
    tokens = tokens_ref[...]
    group = 8
    for start in range(0, EXPERTS, group):
        picks = [
            jnp.where(slot_ids == position[e : e + 1, :], 1.0, 0.0)
            for e in range(start, start + group)
        ]
        pick = jnp.concatenate(picks, axis=0).astype(bf16)
        rows = jnp.dot(pick, tokens, preferred_element_type=f32)
        for i in range(group):
            out_ref[start + i] = rows[i * SLOTS : (i + 1) * SLOTS].astype(bf16)


def pack(routes_t, tokens):
    width = tokens.shape[1]
    return pl.pallas_call(
        pack_kernel,
        out_shape=(
            jax.ShapeDtypeStruct((EXPERTS, SLOTS, width), bf16),
            jax.ShapeDtypeStruct((EXPERTS, TOK), f32),
        ),
        compiler_params=pltpu.CompilerParams(vmem_limit_bytes=VMEM_LIMIT),
        cost_estimate=pl.CostEstimate(flops=300_000_000, bytes_accessed=2_500_000, transcendentals=0),
    )(routes_t, tokens)


def upstream_kernel(rows_ref, down_ref, out_ref):
    out_ref[0] = lax.dot_general(
        rows_ref[...], down_ref[...], (((1,), (1,)), ((), ())), preferred_element_type=f32
    ).astype(bf16)


def upstream_partial(rows, down, parts):
    count, width = rows.shape
    share = down.shape[0] // parts
    return pl.pallas_call(
        upstream_kernel,
        grid=(parts,),
        in_specs=[
            pl.BlockSpec((count, width), lambda g: (0, 0)),
            pl.BlockSpec((share, width), lambda g: (g, 0)),
        ],
        out_specs=pl.BlockSpec((1, count, share), lambda g: (g, 0, 0)),
        out_shape=jax.ShapeDtypeStruct((parts, count, share), bf16),
        compiler_params=pltpu.CompilerParams(vmem_limit_bytes=VMEM_LIMIT),
        cost_estimate=pl.CostEstimate(
            flops=2 * count * width * down.shape[0], bytes_accessed=10_500_000, transcendentals=0
        ),
    )(rows, down)


def back_kernel(hidden_ref, down_ref, out_ref):
    part = jnp.dot(hidden_ref[0], down_ref[...], preferred_element_type=f32)

    @pl.when(pl.program_id(0) == 0)
    def _():
        out_ref[...] = part

    @pl.when(pl.program_id(0) > 0)
    def _():
        out_ref[...] += part


def hidden_times_down(hidden, down):
    parts, count, share = hidden.shape
    width = down.shape[1]
    return pl.pallas_call(
        back_kernel,
        grid=(parts,),
        in_specs=[
            pl.BlockSpec((1, count, share), lambda g: (g, 0, 0)),
            pl.BlockSpec((share, width), lambda g: (g, 0)),
        ],
        out_specs=pl.BlockSpec((count, width), lambda g: (0, 0)),
        out_shape=jax.ShapeDtypeStruct((count, width), f32),
        compiler_params=pltpu.CompilerParams(vmem_limit_bytes=VMEM_LIMIT),
        cost_estimate=pl.CostEstimate(
            flops=2 * count * width * down.shape[0], bytes_accessed=12_500_000, transcendentals=0
        ),
    )(hidden, down)


def grad_down_kernel(hidden_ref, rows_ref, gate_ref, out_ref, scaled_ref):
    @pl.when(pl.program_id(0) == 0)
    def _():
        scaled_ref[...] = (gate_ref[...] * rows_ref[...].astype(f32)).astype(bf16)

    out_ref[0] = lax.dot_general(
        hidden_ref[0], scaled_ref[...], (((0,), (0,)), ((), ())), preferred_element_type=f32
    ).astype(bf16)


def grad_down_of(hidden, rows, gate):
    parts, count, share = hidden.shape
    width = rows.shape[1]
    return pl.pallas_call(
        grad_down_kernel,
        grid=(parts,),
        in_specs=[
            pl.BlockSpec((1, count, share), lambda g: (g, 0, 0)),
            pl.BlockSpec((count, width), lambda g: (0, 0)),
            pl.BlockSpec((count, 1), lambda g: (0, 0)),
        ],
        out_specs=pl.BlockSpec((1, share, width), lambda g: (0, g, 0)),
        out_shape=jax.ShapeDtypeStruct((1, parts * share, width), bf16),
        scratch_shapes=[pltpu.VMEM((count, width), bf16)],
        compiler_params=pltpu.CompilerParams(vmem_limit_bytes=VMEM_LIMIT),
        cost_estimate=pl.CostEstimate(
            flops=2 * count * width * parts * share, bytes_accessed=12_500_000, transcendentals=0
        ),
    )(hidden, rows, gate)


def exchange(value, axes):
    return lax.all_to_all(value, axes, split_axis=0, concat_axis=0, tiled=True)


def spread(value, axes, copies):
    return exchange(jnp.broadcast_to(value[None], (copies,) + value.shape), axes)


def muon(attention):
    mats, latent, width = attention.shape
    got = exchange(attention, "y")
    part = jnp.sum(got.astype(f32), axis=0).astype(bf16)
    got = exchange(part.reshape(8, latent // 8, width), "z")
    part = jnp.sum(got.astype(f32), axis=0).astype(bf16)
    summed = lax.all_gather(part, "z", axis=0, tiled=False).reshape(latent, width)
    gram = lax.dot_general(summed, summed, (((1,), (1,)), ((), ())), preferred_element_type=f32)
    got = exchange(gram.reshape(8, latent // 8, latent), FS)
    gram = spread(jnp.sum(got, axis=0), FS, 8).reshape(latent, latent)
    eye = jnp.eye(latent, dtype=f32)
    norm = jnp.sqrt(jnp.sum(gram * eye)) + NORM_EPS
    inverse = 1.0 / norm
    dot = lambda a, b: jnp.dot(a, b, precision=lax.Precision.HIGHEST)
    first = gram * inverse * inverse
    poly_first = COEF_A * eye + COEF_B * first + COEF_C * dot(first, first)
    second = dot(poly_first, dot(first, poly_first))
    poly_second = COEF_A * eye + COEF_B * second + COEF_C * dot(second, second)
    factor = 0.2 * jnp.sqrt(f32(max(LATENT, D)))
    both = dot(poly_second, poly_first) * (factor * inverse)
    high = both.astype(bf16)
    low = (both - high.astype(f32)).astype(bf16)
    mine = jnp.dot(high, summed, preferred_element_type=f32) + jnp.dot(
        low, summed, preferred_element_type=f32
    )
    return lax.all_gather(mine.astype(bf16), "y", axis=0, tiled=False)


def on_device(
    out_grad,
    router_input,
    router_weight,
    routes,
    balance_grad,
    saved_hidden,
    expert_down,
    attention_grads,
):
    width = out_grad.shape[1]
    down = expert_down[0]
    share = saved_hidden.shape[3]
    count = CAP * EXPERTS
    hidden_share = jnp.swapaxes(saved_hidden[0], 0, 1).reshape(count, share)
    hidden = lax.all_gather(hidden_share, FS, axis=0, tiled=False)

    weight_t = router_weight.T
    input_f = router_input.astype(f32)
    partial_logits = lax.dot_general(
        weight_t, input_f, (((1,), (1,)), ((), ())), precision=lax.Precision.HIGHEST
    )
    packed, position = pack(routes.T, out_grad)
    rows_got = exchange(packed, EP)
    logits = jnp.sum(spread(partial_logits, FS, 8), axis=0)
    muon_update = muon(attention_grads[0])

    scores = jax.nn.sigmoid(logits)
    chosen = position >= 0.0
    selected = chosen.astype(f32)
    score_total = jnp.sum(selected * scores, axis=0, keepdims=True)
    gates = (selected * ROUTE_SCALE * scores / score_total).astype(bf16).astype(f32)
    slot_ids = jnp.arange(SLOTS, dtype=jnp.int32).astype(f32)
    matches = position[:, None, :] == slot_ids[None, :, None]
    slot_gates = jnp.sum(jnp.where(matches, gates[:, None, :], 0.0), axis=2)
    gate_got = exchange(slot_gates, EP)
    gate_column = gate_got[:, :CAP].T.reshape(count, 1)

    rows = jnp.swapaxes(rows_got[:, :CAP], 0, 1).reshape(count, width)
    back = hidden_times_down(hidden, down)
    gate_part = jnp.sum(back * rows.astype(f32), axis=1).reshape(CAP, EXPERTS).T
    returned = exchange(jnp.pad(gate_part, ((0, 0), (0, SLOTS - CAP))), EP)
    back_part = jnp.sum(jnp.where(matches, returned[:, :, None], 0.0), axis=1)
    gate_back = jnp.sum(spread(back_part, FS, 8), axis=0)

    upstream = lax.psum_scatter(
        upstream_partial(rows, down, 8), FS, scatter_dimension=0, tiled=True
    )
    grad_hidden = (gate_column * upstream.reshape(count, share).astype(f32)).astype(bf16)
    grad_hidden = jnp.swapaxes(grad_hidden.reshape(CAP, EXPERTS, share), 0, 1)[None]
    grad_down = grad_down_of(hidden, rows, gate_column)

    weighted = jnp.sum(selected * gate_back * scores, axis=0, keepdims=True) / score_total
    score_grad = balance_grad.T + selected * (ROUTE_SCALE / score_total) * (gate_back - weighted)
    logit_grad = score_grad * scores * (1.0 - scores)
    router_part = jnp.dot(logit_grad, input_f, precision=lax.Precision.HIGHEST)
    router_got = exchange(router_part, EP)
    router_row = jnp.sum(router_got.reshape(EXPERTS, width), axis=0)
    router_grad = spread(router_row.reshape(1, width), EP, EXPERTS).reshape(EXPERTS, width).T
    token_grad = lax.dot_general(
        logit_grad, weight_t, (((0,), (0,)), ((), ())), precision=lax.Precision.HIGHEST
    ).astype(bf16)
    return (grad_hidden, grad_down, router_grad, token_grad, muon_update)


def solution(mesh):
    split = Mesh(mesh.devices.reshape(4, 2, 8, 4), ("x", "c", "z", "y"))
    in_specs = (
        P(EP, FS),
        P(EP, FS),
        P(FS, None),
        P(EP, None),
        P(EP, None),
        P(EP, None, None, FS),
        P(EP, None, FS),
        P(EP, None, None, FS),
    )
    out_specs = (
        P(EP, None, None, FS),
        P(EP, None, FS),
        P(FS, None),
        P(EP, FS),
        P(None, None, FS),
    )
    return jax.shard_map(
        on_device, mesh=split, in_specs=in_specs, out_specs=out_specs, check_vma=False
    )
```

```python
import jax
import jax.numpy as jnp
from jax import lax
from jax.experimental import pallas as pl
from jax.experimental.pallas import tpu as pltpu
from jax.sharding import Mesh, PartitionSpec as P

D = 7168
LATENT = 288
ROUTE_SCALE = 2.827
NORM_EPS = 1e-07
COEF_A = 3.4445
COEF_B = -4.775
COEF_C = 2.0315
CAP = 36
SLOTS = 40
EXPERTS = 32
TOK = 128

FS = ("x", "c")
EP = ("z", "y")
f32 = jnp.float32
bf16 = jnp.bfloat16
VMEM_LIMIT = 48 * 1024 * 1024


def pack_kernel(routes_ref, tokens_ref, input_ref, weight_ref, out_ref, pos_ref, logit_ref):
    expert_ids = lax.broadcasted_iota(jnp.int32, (EXPERTS, TOK), 0)
    chosen = jnp.zeros((EXPERTS, TOK), f32)
    for k in range(routes_ref.shape[0]):
        chosen = chosen + jnp.where(routes_ref[k : k + 1, :] == expert_ids, 1.0, 0.0)
    before = lax.broadcasted_iota(jnp.int32, (TOK, TOK), 0)
    after = lax.broadcasted_iota(jnp.int32, (TOK, TOK), 1)
    upper = jnp.where(before <= after, 1.0, 0.0).astype(bf16)
    counted = jnp.dot(chosen.astype(bf16), upper, preferred_element_type=f32)
    position = jnp.where(chosen > 0.0, counted - 1.0, -1.0)
    pos_ref[...] = position
    slot_ids = lax.broadcasted_iota(jnp.int32, (SLOTS, TOK), 0).astype(f32)
    tokens = tokens_ref[...]
    group = 8
    for start in range(0, EXPERTS, group):
        picks = [
            jnp.where(slot_ids == position[e : e + 1, :], 1.0, 0.0)
            for e in range(start, start + group)
        ]
        pick = jnp.concatenate(picks, axis=0).astype(bf16)
        rows = jnp.dot(pick, tokens, preferred_element_type=f32)
        for i in range(group):
            out_ref[start + i] = rows[i * SLOTS : (i + 1) * SLOTS].astype(bf16)
    rest = weight_ref[...]
    logits = jnp.zeros((EXPERTS, TOK), f32)
    for _ in range(3):
        term = rest.astype(bf16)
        rest = rest - term.astype(f32)
        logits = logits + lax.dot_general(
            term, input_ref[...], (((1,), (1,)), ((), ())), preferred_element_type=f32
        )
    logit_ref[...] = logits


def pack(routes_t, tokens, router_input, weight_t):
    width = tokens.shape[1]
    return pl.pallas_call(
        pack_kernel,
        out_shape=(
            jax.ShapeDtypeStruct((EXPERTS, SLOTS, width), bf16),
            jax.ShapeDtypeStruct((EXPERTS, TOK), f32),
            jax.ShapeDtypeStruct((EXPERTS, TOK), f32),
        ),
        compiler_params=pltpu.CompilerParams(vmem_limit_bytes=VMEM_LIMIT),
        cost_estimate=pl.CostEstimate(flops=300_000_000, bytes_accessed=2_800_000, transcendentals=0),
    )(routes_t, tokens, router_input, weight_t)


def upstream_kernel(rows_ref, down_ref, after_ref, out_ref):
    out_ref[0] = lax.dot_general(
        rows_ref[...], down_ref[...], (((1,), (1,)), ((), ())), preferred_element_type=f32
    ).astype(bf16)


def upstream_partial(rows, down, after, parts):
    count, width = rows.shape
    share = down.shape[0] // parts
    return pl.pallas_call(
        upstream_kernel,
        grid=(parts,),
        in_specs=[
            pl.BlockSpec((count, width), lambda g: (0, 0)),
            pl.BlockSpec((share, width), lambda g: (g, 0)),
            AFTER,
        ],
        out_specs=pl.BlockSpec((1, count, share), lambda g: (g, 0, 0)),
        out_shape=jax.ShapeDtypeStruct((parts, count, share), bf16),
        compiler_params=pltpu.CompilerParams(vmem_limit_bytes=VMEM_LIMIT),
        cost_estimate=pl.CostEstimate(
            flops=2 * count * width * down.shape[0], bytes_accessed=10_500_000, transcendentals=0
        ),
    )(rows, down, after)


def back_kernel(hidden_ref, down_ref, out_ref):
    part = jnp.dot(hidden_ref[0], down_ref[...], preferred_element_type=f32)

    @pl.when(pl.program_id(0) == 0)
    def _():
        out_ref[...] = part

    @pl.when(pl.program_id(0) > 0)
    def _():
        out_ref[...] += part


def hidden_times_down(hidden, down):
    parts, count, share = hidden.shape
    width = down.shape[1]
    return pl.pallas_call(
        back_kernel,
        grid=(parts,),
        in_specs=[
            pl.BlockSpec((1, count, share), lambda g: (g, 0, 0)),
            pl.BlockSpec((share, width), lambda g: (g, 0)),
        ],
        out_specs=pl.BlockSpec((count, width), lambda g: (0, 0)),
        out_shape=jax.ShapeDtypeStruct((count, width), f32),
        compiler_params=pltpu.CompilerParams(vmem_limit_bytes=VMEM_LIMIT),
        cost_estimate=pl.CostEstimate(
            flops=2 * count * width * down.shape[0], bytes_accessed=12_500_000, transcendentals=0
        ),
    )(hidden, down)


def grad_down_kernel(hidden_ref, rows_ref, gate_ref, out_ref, scaled_ref):
    @pl.when(pl.program_id(0) == 0)
    def _():
        scaled_ref[...] = (gate_ref[...] * rows_ref[...].astype(f32)).astype(bf16)

    out_ref[0] = lax.dot_general(
        hidden_ref[0], scaled_ref[...], (((0,), (0,)), ((), ())), preferred_element_type=f32
    ).astype(bf16)


def grad_down_of(hidden, rows, gate):
    parts, count, share = hidden.shape
    width = rows.shape[1]
    return pl.pallas_call(
        grad_down_kernel,
        grid=(parts,),
        in_specs=[
            pl.BlockSpec((1, count, share), lambda g: (g, 0, 0)),
            pl.BlockSpec((count, width), lambda g: (0, 0)),
            pl.BlockSpec((count, 1), lambda g: (0, 0)),
        ],
        out_specs=pl.BlockSpec((1, share, width), lambda g: (0, g, 0)),
        out_shape=jax.ShapeDtypeStruct((1, parts * share, width), bf16),
        scratch_shapes=[pltpu.VMEM((count, width), bf16)],
        compiler_params=pltpu.CompilerParams(vmem_limit_bytes=VMEM_LIMIT),
        cost_estimate=pl.CostEstimate(
            flops=2 * count * width * parts * share, bytes_accessed=12_500_000, transcendentals=0
        ),
    )(hidden, rows, gate)


def exchange(value, axes):
    return lax.all_to_all(value, axes, split_axis=0, concat_axis=0, tiled=True)


def spread(value, axes, copies):
    return exchange(jnp.broadcast_to(value[None], (copies,) + value.shape), axes)


def swap(pieces, axes, size):
    got = [pieces[0]]
    for k in range(1, size):
        got.append(lax.ppermute(pieces[k], axes, [(i, (i + k) % size) for i in range(size)]))
    return got


def total_of(pieces):
    total = pieces[0].astype(f32)
    for piece in pieces[1:]:
        total = total + piece.astype(f32)
    return total


BLOCK = 40
PADDED = 8 * BLOCK
SHARE = LATENT // 8


def cut_kernel(z_ref, *refs):
    parts, outs = refs[:4], refs[4:]
    total = total_of([part[...] for part in parts]).astype(bf16)
    row = lax.broadcasted_iota(jnp.int32, (PADDED, LATENT), 0)
    column = lax.broadcasted_iota(jnp.int32, (PADDED, LATENT), 1)
    shift = row // BLOCK
    within = row - shift * BLOCK
    block = shift + z_ref[0]
    block = jnp.where(block >= 8, block - 8, block)
    source = jnp.where(within < SHARE, block * SHARE + within, -1)
    pick = jnp.where(source == column, 1.0, 0.0).astype(bf16)
    rows = jnp.dot(pick, total, preferred_element_type=f32)
    for k in range(8):
        outs[k][...] = rows[k * BLOCK : (k + 1) * BLOCK].astype(bf16)


def gram_kernel(f_ref, *refs):
    parts, whole_ref, outs, scratch = refs[:8], refs[10], refs[11:19], refs[19]
    whole = jnp.concatenate([part[...].astype(f32) for part in parts], axis=0).astype(bf16)
    whole_ref[...] = whole
    scratch[...] = lax.dot_general(
        whole, whole, (((1,), (1,)), ((), ())), preferred_element_type=f32
    )
    for k in range(8):
        block = lax.rem(f_ref[0] + k, 8)
        outs[k][...] = scratch[pl.ds(pl.multiple_of(block * BLOCK, 8), BLOCK), :]


def newton_kernel(place_ref, *refs):
    parts, whole_ref, out_ref, scratch = refs[:8], refs[8], refs[10], refs[11]
    for k in range(8):
        block = lax.rem(place_ref[0] + 8 - k, 8)
        scratch[pl.ds(pl.multiple_of(block * BLOCK, 8), BLOCK), :] = parts[k][...]
    gram = scratch[...]
    row = lax.broadcasted_iota(jnp.int32, (PADDED, PADDED), 0)
    column = lax.broadcasted_iota(jnp.int32, (PADDED, PADDED), 1)
    eye = jnp.where(row == column, 1.0, 0.0)
    squares = jnp.sum(jnp.sum(gram * eye, axis=1, keepdims=True), axis=0, keepdims=True)
    inverse = 1.0 / (jnp.sqrt(squares) + NORM_EPS)
    dot = lambda a, b: jnp.dot(
        a, b, precision=lax.Precision.HIGHEST, preferred_element_type=f32
    )
    first = gram * inverse * inverse
    poly_first = COEF_A * eye + COEF_B * first + COEF_C * dot(first, first)
    second = dot(poly_first, dot(first, poly_first))
    poly_second = COEF_A * eye + COEF_B * second + COEF_C * dot(second, second)
    factor = 0.2 * float(D) ** 0.5
    both = dot(poly_second, poly_first) * (factor * inverse)
    shift = row // BLOCK
    within = row - shift * BLOCK
    block = place_ref[1] - shift
    block = jnp.where(block < 0, block + 8, block)
    target = jnp.where(within < SHARE, block * SHARE + within, -1)
    pick_t = jnp.where(target == column, 1.0, 0.0)
    both = lax.dot_general(
        pick_t,
        both,
        (((0,), (0,)), ((), ())),
        precision=lax.Precision.HIGHEST,
        preferred_element_type=f32,
    )[:LATENT]
    high = both.astype(bf16)
    low = (both - high.astype(f32)).astype(bf16)
    whole = whole_ref[...]
    out_ref[...] = (
        jnp.dot(high, whole, preferred_element_type=f32)
        + jnp.dot(low, whole, preferred_element_type=f32)
    ).astype(bf16)


SMEM = pl.BlockSpec(memory_space=pltpu.SMEM)
WHOLE = pl.BlockSpec(memory_space=pltpu.VMEM)


PIECE = jax.ShapeDtypeStruct((BLOCK, D // 8), bf16)
SQUARE_PIECE = jax.ShapeDtypeStruct((BLOCK, PADDED), f32)
AFTER = pl.BlockSpec(memory_space=pl.ANY)
PARAMS = pltpu.CompilerParams(vmem_limit_bytes=VMEM_LIMIT)


def muon_sum(attention, after):
    y_at = lax.axis_index("y")
    mine = [
        lax.dynamic_index_in_dim(attention, lax.rem(y_at + k, 4), 0, keepdims=False)
        for k in range(4)
    ]
    blocks = pl.pallas_call(
        cut_kernel,
        in_specs=[SMEM] + [WHOLE] * 4,
        out_specs=[WHOLE] * 8,
        out_shape=[PIECE] * 8,
        compiler_params=PARAMS,
        cost_estimate=pl.CostEstimate(flops=170_000_000, bytes_accessed=2_700_000, transcendentals=0),
    )(lax.axis_index("z")[None], *swap(mine, "y", 4))
    row_block = total_of(swap(blocks, "z", 8)).astype(bf16)
    gathered = swap([row_block] * 8, "z", 8)
    whole, *squares = pl.pallas_call(
        gram_kernel,
        in_specs=[SMEM] + [WHOLE] * 8 + [AFTER] * 2,
        out_specs=[WHOLE] * 9,
        out_shape=[jax.ShapeDtypeStruct((PADDED, D // 8), bf16)] + [SQUARE_PIECE] * 8,
        scratch_shapes=[pltpu.VMEM((PADDED, PADDED), f32)],
        compiler_params=PARAMS,
        cost_estimate=pl.CostEstimate(flops=180_000_000, bytes_accessed=1_600_000, transcendentals=0),
    )(lax.axis_index(FS)[None], *gathered, *after)
    return whole, squares


def muon_update_of(whole, gram_parts, after):
    place = jnp.stack([lax.axis_index(FS), lax.axis_index("z")])
    return pl.pallas_call(
        newton_kernel,
        in_specs=[SMEM] + [WHOLE] * 9 + [AFTER],
        out_specs=WHOLE,
        out_shape=jax.ShapeDtypeStruct((LATENT, D // 8), bf16),
        scratch_shapes=[pltpu.VMEM((PADDED, PADDED), f32)],
        compiler_params=PARAMS,
        cost_estimate=pl.CostEstimate(
            flops=3_000_000_000, bytes_accessed=1_600_000, transcendentals=0
        ),
    )(place, *gram_parts, whole, after)


def muon_spread(update):
    y_at = lax.axis_index("y")
    out = jnp.zeros((4,) + update.shape, bf16)
    for k, got in enumerate(swap([update] * 4, "y", 4)):
        out = lax.dynamic_update_index_in_dim(out, got, lax.rem(y_at + 4 - k, 4), 0)
    return out


def join_kernel(first_ref, second_ref, after_ref, out_ref):
    out_ref[:, 0, :] = first_ref[...]
    out_ref[:, 1, :] = second_ref[...]


def join(first, second, after):
    return pl.pallas_call(
        join_kernel,
        in_specs=[WHOLE, WHOLE, AFTER],
        out_specs=WHOLE,
        out_shape=jax.ShapeDtypeStruct((first.shape[0], 2, first.shape[1]), f32),
        compiler_params=PARAMS,
    )(first, second, after)


def hand_kernel(value_ref, after_ref, out_ref):
    out_ref[...] = value_ref[...]


def hand(value, after):
    return pl.pallas_call(
        hand_kernel,
        in_specs=[WHOLE, AFTER],
        out_specs=WHOLE,
        out_shape=jax.ShapeDtypeStruct(value.shape, value.dtype),
        compiler_params=PARAMS,
    )(value, after)


def add_kernel(values_ref, after_ref, out_ref):
    total = values_ref[0]
    for i in range(1, values_ref.shape[0]):
        total = total + values_ref[i]
    out_ref[...] = total


def add_up(values, after):
    return pl.pallas_call(
        add_kernel,
        in_specs=[WHOLE, AFTER],
        out_specs=WHOLE,
        out_shape=jax.ShapeDtypeStruct(values.shape[1:], values.dtype),
        compiler_params=PARAMS,
    )(values, after)


def on_device(
    out_grad,
    router_input,
    router_weight,
    routes,
    balance_grad,
    saved_hidden,
    expert_down,
    attention_grads,
):
    width = out_grad.shape[1]
    down = expert_down[0]
    share = saved_hidden.shape[3]
    count = CAP * EXPERTS
    hidden_share = jnp.swapaxes(saved_hidden[0], 0, 1).reshape(count, share)
    hidden = lax.all_gather(hidden_share, FS, axis=0, tiled=False)

    weight_t = router_weight.T
    input_f = router_input.astype(f32)
    packed, position, partial_logits = pack(routes.T, out_grad, router_input, weight_t)
    rows_got = exchange(packed, EP)
    logits = total_of(swap([partial_logits] * 8, FS, 8))

    scores = jax.nn.sigmoid(logits)
    chosen = position >= 0.0
    selected = chosen.astype(f32)
    score_total = jnp.sum(selected * scores, axis=0, keepdims=True)
    gates = (selected * ROUTE_SCALE * scores / score_total).astype(bf16).astype(f32)
    slot_ids = jnp.arange(SLOTS, dtype=jnp.int32).astype(f32)
    matches = position[:, None, :] == slot_ids[None, :, None]
    slot_gates = jnp.sum(jnp.where(matches, gates[:, None, :], 0.0), axis=2)
    back = hidden_times_down(hidden, down)
    whole, squares = muon_sum(attention_grads[0], (back, slot_gates))
    keep = jnp.where(whole[0, 0] < f32(jnp.inf), 1.0, 0.0).astype(bf16)
    rows = jnp.swapaxes(rows_got[:, :CAP] * keep, 0, 1).reshape(count, width)
    gate_part = jnp.sum(back * rows.astype(f32), axis=1)
    gate_part_t = jnp.pad(gate_part.reshape(CAP, EXPERTS).T, ((0, 0), (0, SLOTS - CAP)))
    joined = join(slot_gates, gate_part_t, whole)
    both_got = exchange(joined, EP)
    square_block = total_of(swap(squares, FS, 8))
    gate_column = both_got[:, 0, :CAP].T.reshape(count, 1)
    returned = both_got[:, 1]
    back_part = jnp.sum(jnp.where(matches, returned[:, :, None], 0.0), axis=1)
    gram_parts = swap([square_block] * 8, FS, 8)
    grad_down = grad_down_of(hidden, rows, gate_column)
    back_parts = spread(hand(back_part, square_block), FS, 8)
    gate_back = add_up(back_parts, grad_down)

    upstream = lax.psum_scatter(
        upstream_partial(rows, down, joined, 8), FS, scatter_dimension=0, tiled=True
    )
    grad_hidden = (gate_column * upstream.reshape(count, share).astype(f32)).astype(bf16)
    grad_hidden = jnp.swapaxes(grad_hidden.reshape(CAP, EXPERTS, share), 0, 1)[None]

    weighted = jnp.sum(selected * gate_back * scores, axis=0, keepdims=True) / score_total
    score_grad = balance_grad.T + selected * (ROUTE_SCALE / score_total) * (gate_back - weighted)
    logit_grad = score_grad * scores * (1.0 - scores)
    router_part = jnp.dot(logit_grad, input_f, precision=lax.Precision.HIGHEST)
    router_got = exchange(router_part.reshape(EXPERTS, 1, width), EP)
    update = muon_update_of(whole, gram_parts, router_part)
    muon_update = muon_spread(update)
    router_row = add_up(router_got, update)
    router_grad = spread(router_row, EP, EXPERTS).reshape(EXPERTS, width).T
    token_grad = lax.dot_general(
        logit_grad, weight_t, (((0,), (0,)), ((), ())), precision=lax.Precision.HIGHEST
    ).astype(bf16)
    return (grad_hidden, grad_down, router_grad, token_grad, muon_update)


def solution(mesh):
    split = Mesh(mesh.devices.reshape(4, 2, 8, 4), ("x", "c", "z", "y"))
    in_specs = (
        P(EP, FS),
        P(EP, FS),
        P(FS, None),
        P(EP, None),
        P(EP, None),
        P(EP, None, None, FS),
        P(EP, None, FS),
        P(EP, None, None, FS),
    )
    out_specs = (
        P(EP, None, None, FS),
        P(EP, None, FS),
        P(FS, None),
        P(EP, FS),
        P(None, None, FS),
    )
    return jax.shard_map(
        on_device, mesh=split, in_specs=in_specs, out_specs=out_specs, check_vma=False
    )
```

```python
import jax
import jax.numpy as jnp
from jax import lax
from jax.experimental import pallas as pl
from jax.experimental.pallas import tpu as pltpu
from jax.sharding import Mesh, PartitionSpec as P

D = 7168
LATENT = 288
ROUTE_SCALE = 2.827
NORM_EPS = 1e-07
COEF_A = 3.4445
COEF_B = -4.775
COEF_C = 2.0315
CAP = 36
SLOTS = 40
EXPERTS = 32
TOK = 128

FS = ("x", "c")
EP = ("z", "y")
f32 = jnp.float32
bf16 = jnp.bfloat16
VMEM_LIMIT = 48 * 1024 * 1024


def pack_kernel(routes_ref, tokens_ref, input_ref, weight_ref, out_ref, pos_ref, logit_ref):
    expert_ids = lax.broadcasted_iota(jnp.int32, (EXPERTS, TOK), 0)
    chosen = jnp.zeros((EXPERTS, TOK), f32)
    for k in range(routes_ref.shape[0]):
        chosen = chosen + jnp.where(routes_ref[k : k + 1, :] == expert_ids, 1.0, 0.0)
    before = lax.broadcasted_iota(jnp.int32, (TOK, TOK), 0)
    after = lax.broadcasted_iota(jnp.int32, (TOK, TOK), 1)
    upper = jnp.where(before <= after, 1.0, 0.0).astype(bf16)
    counted = jnp.dot(chosen.astype(bf16), upper, preferred_element_type=f32)
    position = jnp.where(chosen > 0.0, counted - 1.0, -1.0)
    pos_ref[...] = position
    slot_ids = lax.broadcasted_iota(jnp.int32, (SLOTS, TOK), 0).astype(f32)
    tokens = tokens_ref[...]
    group = 8
    for start in range(0, EXPERTS, group):
        picks = [
            jnp.where(slot_ids == position[e : e + 1, :], 1.0, 0.0)
            for e in range(start, start + group)
        ]
        pick = jnp.concatenate(picks, axis=0).astype(bf16)
        rows = jnp.dot(pick, tokens, preferred_element_type=f32)
        for i in range(group):
            out_ref[start + i] = rows[i * SLOTS : (i + 1) * SLOTS].astype(bf16)
    rest = weight_ref[...]
    logits = jnp.zeros((EXPERTS, TOK), f32)
    for _ in range(3):
        term = rest.astype(bf16)
        rest = rest - term.astype(f32)
        logits = logits + lax.dot_general(
            term, input_ref[...], (((1,), (1,)), ((), ())), preferred_element_type=f32
        )
    logit_ref[...] = logits


def pack(routes_t, tokens, router_input, weight_t):
    width = tokens.shape[1]
    return pl.pallas_call(
        pack_kernel,
        out_shape=(
            jax.ShapeDtypeStruct((EXPERTS, SLOTS, width), bf16),
            jax.ShapeDtypeStruct((EXPERTS, TOK), f32),
            jax.ShapeDtypeStruct((EXPERTS, TOK), f32),
        ),
        compiler_params=pltpu.CompilerParams(vmem_limit_bytes=VMEM_LIMIT),
        cost_estimate=pl.CostEstimate(flops=300_000_000, bytes_accessed=2_800_000, transcendentals=0),
    )(routes_t, tokens, router_input, weight_t)


def upstream_kernel(first_ref, rows_ref, down_ref, *refs):
    refs[-1][0] = lax.dot_general(
        rows_ref[...], down_ref[...], (((1,), (1,)), ((), ())), preferred_element_type=f32
    ).astype(bf16)


def upstream_partial(rows, down, place, core, after):
    count, width = rows.shape
    share = down.shape[0] // 8
    grid_spec = pltpu.PrefetchScalarGridSpec(
        num_scalar_prefetch=1,
        grid=(4,),
        in_specs=[
            pl.BlockSpec((count, width), lambda g, p: (0, 0)),
            pl.BlockSpec((share, width), lambda g, p: (2 * lax.rem(p[0] + g, 4) + p[1], 0)),
            pl.BlockSpec(memory_space=pl.ANY),
        ],
        out_specs=pl.BlockSpec((1, count, share), lambda g, p: (g, 0, 0)),
    )
    return pl.pallas_call(
        upstream_kernel,
        grid_spec=grid_spec,
        out_shape=jax.ShapeDtypeStruct((4, count, share), bf16),
        compiler_params=pltpu.CompilerParams(vmem_limit_bytes=VMEM_LIMIT),
        cost_estimate=pl.CostEstimate(
            flops=count * width * down.shape[0], bytes_accessed=6_300_000, transcendentals=0
        ),
    )(jnp.stack([place, core]), rows, down, after)


def back_kernel(hidden_ref, down_ref, out_ref):
    parts = hidden_ref.shape[0]
    whole = jnp.concatenate([hidden_ref[g] for g in range(parts)], axis=1)
    out_ref[...] = jnp.dot(whole, down_ref[...], preferred_element_type=f32)


def hidden_times_down(hidden, down):
    parts, count, share = hidden.shape
    width = down.shape[1]
    steps = 4
    block = count // steps
    return pl.pallas_call(
        back_kernel,
        grid=(steps,),
        in_specs=[
            pl.BlockSpec((parts, block, share), lambda g: (0, g, 0)),
            pl.BlockSpec((parts * share, width), lambda g: (0, 0)),
        ],
        out_specs=pl.BlockSpec((block, width), lambda g: (g, 0)),
        out_shape=jax.ShapeDtypeStruct((count, width), f32),
        compiler_params=pltpu.CompilerParams(vmem_limit_bytes=VMEM_LIMIT),
        cost_estimate=pl.CostEstimate(
            flops=2 * count * width * down.shape[0], bytes_accessed=12_500_000, transcendentals=0
        ),
    )(hidden, down)


def grad_down_kernel(hidden_ref, rows_ref, gate_ref, out_ref, scaled_ref):
    @pl.when(pl.program_id(0) == 0)
    def _():
        scaled_ref[...] = (gate_ref[...] * rows_ref[...].astype(f32)).astype(bf16)

    out_ref[0] = lax.dot_general(
        hidden_ref[0], scaled_ref[...], (((0,), (0,)), ((), ())), preferred_element_type=f32
    ).astype(bf16)


def grad_down_of(hidden, rows, gate):
    parts, count, share = hidden.shape
    width = rows.shape[1]
    return pl.pallas_call(
        grad_down_kernel,
        grid=(parts,),
        in_specs=[
            pl.BlockSpec((1, count, share), lambda g: (g, 0, 0)),
            pl.BlockSpec((count, width), lambda g: (0, 0)),
            pl.BlockSpec((count, 1), lambda g: (0, 0)),
        ],
        out_specs=pl.BlockSpec((1, share, width), lambda g: (0, g, 0)),
        out_shape=jax.ShapeDtypeStruct((1, parts * share, width), bf16),
        scratch_shapes=[pltpu.VMEM((count, width), bf16)],
        compiler_params=pltpu.CompilerParams(vmem_limit_bytes=VMEM_LIMIT),
        cost_estimate=pl.CostEstimate(
            flops=2 * count * width * parts * share, bytes_accessed=12_500_000, transcendentals=0
        ),
    )(hidden, rows, gate)


def exchange(value, axes):
    return lax.all_to_all(value, axes, split_axis=0, concat_axis=0, tiled=True)


def spread(value, axes, copies):
    return exchange(jnp.broadcast_to(value[None], (copies,) + value.shape), axes)


def swap(pieces, axes, size):
    got = [pieces[0]]
    for k in range(1, size):
        got.append(lax.ppermute(pieces[k], axes, [(i, (i + k) % size) for i in range(size)]))
    return got


def total_of(pieces):
    total = pieces[0].astype(f32)
    for piece in pieces[1:]:
        total = total + piece.astype(f32)
    return total


BLOCK = 40
PADDED = 8 * BLOCK
SHARE = LATENT // 8


def cut_kernel(z_ref, *refs):
    total, outs = refs[0][...], refs[2:]
    row = lax.broadcasted_iota(jnp.int32, (PADDED, LATENT), 0)
    column = lax.broadcasted_iota(jnp.int32, (PADDED, LATENT), 1)
    shift = row // BLOCK
    within = row - shift * BLOCK
    block = shift + z_ref[0]
    block = jnp.where(block >= 8, block - 8, block)
    source = jnp.where(within < SHARE, block * SHARE + within, -1)
    pick = jnp.where(source == column, 1.0, 0.0).astype(bf16)
    rows = jnp.dot(pick, total, preferred_element_type=f32)
    for k in range(8):
        outs[k][...] = rows[k * BLOCK : (k + 1) * BLOCK].astype(bf16)


def gram_kernel(z_ref, *refs):
    parts, whole_ref, gram_ref = refs[:8], refs[9], refs[10]
    rows = jnp.concatenate([part[...].astype(f32) for part in parts], axis=0).astype(bf16)
    row = lax.broadcasted_iota(jnp.int32, (LATENT, PADDED), 0)
    column = lax.broadcasted_iota(jnp.int32, (LATENT, PADDED), 1)
    shift = column // BLOCK
    within = column - shift * BLOCK
    block = z_ref[0] - shift
    block = jnp.where(block < 0, block + 8, block)
    target = jnp.where(within < SHARE, block * SHARE + within, -1)
    pick = jnp.where(target == row, 1.0, 0.0).astype(bf16)
    whole = jnp.dot(pick, rows, preferred_element_type=f32).astype(bf16)
    whole_ref[...] = whole
    gram_ref[...] = lax.dot_general(
        whole, whole, (((1,), (1,)), ((), ())), preferred_element_type=f32
    )


def newton_kernel(grams_ref, whole_ref, after_ref, out_ref):
    gram = total_of([grams_ref[g] for g in range(grams_ref.shape[0])])
    row = lax.broadcasted_iota(jnp.int32, (LATENT, LATENT), 0)
    column = lax.broadcasted_iota(jnp.int32, (LATENT, LATENT), 1)
    eye = jnp.where(row == column, 1.0, 0.0)
    squares = jnp.sum(jnp.sum(gram * eye, axis=1, keepdims=True), axis=0, keepdims=True)
    inverse = 1.0 / (jnp.sqrt(squares) + NORM_EPS)
    dot = lambda a, b: jnp.dot(
        a, b, precision=lax.Precision.HIGHEST, preferred_element_type=f32
    )
    first = gram * inverse * inverse
    poly_first = COEF_A * eye + COEF_B * first + COEF_C * dot(first, first)
    second = dot(poly_first, dot(first, poly_first))
    poly_second = COEF_A * eye + COEF_B * second + COEF_C * dot(second, second)
    factor = 0.2 * float(D) ** 0.5
    both = dot(poly_second, poly_first) * (factor * inverse)
    high = both.astype(bf16)
    low = (both - high.astype(f32)).astype(bf16)
    whole = whole_ref[...]
    out_ref[...] = (
        jnp.dot(high, whole, preferred_element_type=f32)
        + jnp.dot(low, whole, preferred_element_type=f32)
    ).astype(bf16)


SMEM = pl.BlockSpec(memory_space=pltpu.SMEM)
WHOLE = pl.BlockSpec(memory_space=pltpu.VMEM)


PIECE = jax.ShapeDtypeStruct((BLOCK, D // 8), bf16)
AFTER = pl.BlockSpec(memory_space=pl.ANY)
PARAMS = pltpu.CompilerParams(vmem_limit_bytes=VMEM_LIMIT)


def muon_blocks(attention, after):
    part = lax.psum_scatter(attention, "y", scatter_dimension=0, tiled=True)[0]
    blocks = pl.pallas_call(
        cut_kernel,
        in_specs=[SMEM, WHOLE, AFTER],
        out_specs=[WHOLE] * 8,
        out_shape=[PIECE] * 8,
        compiler_params=PARAMS,
        cost_estimate=pl.CostEstimate(flops=170_000_000, bytes_accessed=1_200_000, transcendentals=0),
    )(lax.axis_index("z")[None], part, after)
    return total_of(swap(blocks, "z", 8)).astype(bf16)


def muon_gram(row_block, after):
    gathered = swap([row_block] * 8, "z", 8)
    return pl.pallas_call(
        gram_kernel,
        in_specs=[SMEM] + [WHOLE] * 8 + [AFTER],
        out_specs=[WHOLE] * 2,
        out_shape=[
            jax.ShapeDtypeStruct((LATENT, D // 8), bf16),
            jax.ShapeDtypeStruct((LATENT, LATENT), f32),
        ],
        compiler_params=PARAMS,
        cost_estimate=pl.CostEstimate(flops=300_000_000, bytes_accessed=1_600_000, transcendentals=0),
    )(lax.axis_index("z")[None], *gathered, after)


def muon_update_of(whole, grams, after):
    return pl.pallas_call(
        newton_kernel,
        in_specs=[WHOLE, WHOLE, AFTER],
        out_specs=WHOLE,
        out_shape=jax.ShapeDtypeStruct((LATENT, D // 8), bf16),
        compiler_params=PARAMS,
        cost_estimate=pl.CostEstimate(
            flops=3_000_000_000, bytes_accessed=3_600_000, transcendentals=0
        ),
    )(grams, whole, after)


def muon_spread(update):
    y_at = lax.axis_index("y")
    out = jnp.zeros((4,) + update.shape, bf16)
    for k, got in enumerate(swap([update] * 4, "y", 4)):
        out = lax.dynamic_update_index_in_dim(out, got, lax.rem(y_at + 4 - k, 4), 0)
    return out


def join_kernel(first_ref, second_ref, after_ref, out_ref):
    out_ref[:, 0, :] = first_ref[...]
    out_ref[:, 1, :] = second_ref[...]


def join(first, second, after):
    return pl.pallas_call(
        join_kernel,
        in_specs=[WHOLE, WHOLE, AFTER],
        out_specs=WHOLE,
        out_shape=jax.ShapeDtypeStruct((first.shape[0], 2, first.shape[1]), f32),
        compiler_params=PARAMS,
    )(first, second, after)


def hand_kernel(value_ref, *refs):
    refs[-1][...] = value_ref[...]


def hand(value, *after):
    return pl.pallas_call(
        hand_kernel,
        in_specs=[WHOLE] + [AFTER] * len(after),
        out_specs=WHOLE,
        out_shape=jax.ShapeDtypeStruct(value.shape, value.dtype),
        compiler_params=PARAMS,
    )(value, *after)


def add_kernel(values_ref, after_ref, out_ref):
    total = values_ref[0]
    for i in range(1, values_ref.shape[0]):
        total = total + values_ref[i]
    out_ref[...] = total


def add_up(values, after):
    return pl.pallas_call(
        add_kernel,
        in_specs=[WHOLE, AFTER],
        out_specs=WHOLE,
        out_shape=jax.ShapeDtypeStruct(values.shape[1:], values.dtype),
        compiler_params=PARAMS,
    )(values, after)


def on_device(
    out_grad,
    router_input,
    router_weight,
    routes,
    balance_grad,
    saved_hidden,
    expert_down,
    attention_grads,
):
    width = out_grad.shape[1]
    down = expert_down[0]
    share = saved_hidden.shape[3]
    count = CAP * EXPERTS
    weight_t = router_weight.T
    input_f = router_input.astype(f32)
    packed, position, partial_logits = pack(routes.T, out_grad, router_input, weight_t)
    rows_got = exchange(packed, EP)
    hidden_share = jnp.swapaxes(saved_hidden[0], 0, 1).reshape(count, share)
    hidden = lax.all_gather(hand(hidden_share, position), FS, axis=0, tiled=False)
    logits = total_of(swap([partial_logits] * 8, FS, 8))

    scores = jax.nn.sigmoid(logits)
    chosen = position >= 0.0
    selected = chosen.astype(f32)
    score_total = jnp.sum(selected * scores, axis=0, keepdims=True)
    gates = (selected * ROUTE_SCALE * scores / score_total).astype(bf16).astype(f32)
    slot_ids = jnp.arange(SLOTS, dtype=jnp.int32).astype(f32)
    matches = position[:, None, :] == slot_ids[None, :, None]
    slot_gates = jnp.sum(jnp.where(matches, gates[:, None, :], 0.0), axis=2)
    back = hidden_times_down(hidden, down)
    row_block = muon_blocks(attention_grads[0], slot_gates)
    ready = (row_block[0, 0] < f32(jnp.inf)) & (back[0, 0] < f32(jnp.inf))
    keep = jnp.where(ready, 1.0, 0.0).astype(bf16)
    rows = jnp.swapaxes(rows_got[:, :CAP] * keep, 0, 1).reshape(count, width)
    whole, gram = muon_gram(row_block, back)
    grams = lax.all_gather(gram, FS, axis=0, tiled=False)
    gate_part = jnp.sum(back * rows.astype(f32), axis=1)
    gate_part_t = jnp.pad(gate_part.reshape(CAP, EXPERTS).T, ((0, 0), (0, SLOTS - CAP)))
    joined = join(slot_gates, gate_part_t, position)
    both_got = exchange(joined, EP)
    gate_column = both_got[:, 0, :CAP].T.reshape(count, 1)
    returned = both_got[:, 1]
    back_part = jnp.sum(jnp.where(matches, returned[:, :, None], 0.0), axis=1)
    grad_down = grad_down_of(hidden, rows, gate_column)
    x_at, core_at = lax.axis_index("x"), lax.axis_index("c")
    for_other = upstream_partial(rows, down, x_at, 1 - core_at, joined)
    from_other = lax.ppermute(for_other, "c", [(0, 1), (1, 0)])
    for_own = upstream_partial(rows, down, x_at, core_at, for_other)
    both_cores = (from_other.astype(f32) + for_own.astype(f32)).astype(bf16)
    upstream = total_of(swap([both_cores[k] for k in range(4)], "x", 4))
    back_parts = spread(hand(back_part, gram, for_own), FS, 8)
    gate_back = add_up(back_parts, grad_down)

    grad_hidden = (gate_column * upstream).astype(bf16)
    grad_hidden = jnp.swapaxes(grad_hidden.reshape(CAP, EXPERTS, share), 0, 1)[None]

    weighted = jnp.sum(selected * gate_back * scores, axis=0, keepdims=True) / score_total
    score_grad = balance_grad.T + selected * (ROUTE_SCALE / score_total) * (gate_back - weighted)
    logit_grad = score_grad * scores * (1.0 - scores)
    router_part = jnp.dot(logit_grad, input_f, precision=lax.Precision.HIGHEST)
    router_got = exchange(router_part.reshape(EXPERTS, 1, width), EP)
    update = muon_update_of(whole, grams, router_part)
    muon_update = muon_spread(update)
    router_row = add_up(router_got, update)
    router_grad = spread(router_row, EP, EXPERTS).reshape(EXPERTS, width).T
    token_grad = lax.dot_general(
        logit_grad, weight_t, (((0,), (0,)), ((), ())), precision=lax.Precision.HIGHEST
    ).astype(bf16)
    return (grad_hidden, grad_down, router_grad, token_grad, muon_update)


def solution(mesh):
    split = Mesh(mesh.devices.reshape(4, 2, 8, 4), ("x", "c", "z", "y"))
    in_specs = (
        P(EP, FS),
        P(EP, FS),
        P(FS, None),
        P(EP, None),
        P(EP, None),
        P(EP, None, None, FS),
        P(EP, None, FS),
        P(EP, None, None, FS),
    )
    out_specs = (
        P(EP, None, None, FS),
        P(EP, None, FS),
        P(FS, None),
        P(EP, FS),
        P(None, None, FS),
    )
    return jax.shard_map(
        on_device, mesh=split, in_specs=in_specs, out_specs=out_specs, check_vma=False
    )
```

```python
import jax
import jax.numpy as jnp
from jax import lax
from jax.experimental import pallas as pl
from jax.experimental.pallas import tpu as pltpu
from jax.sharding import Mesh, PartitionSpec as P

D = 7168
LATENT = 288
ROUTE_SCALE = 2.827
NORM_EPS = 1e-07
COEF_A = 3.4445
COEF_B = -4.775
COEF_C = 2.0315
CAP = 36
SLOTS = 40
EXPERTS = 32
TOK = 128

FS = ("x", "c")
EP = ("z", "y")
f32 = jnp.float32
bf16 = jnp.bfloat16
VMEM_LIMIT = 48 * 1024 * 1024


def pack_kernel(routes_ref, tokens_ref, input_ref, weight_ref, out_ref, pos_ref, logit_ref):
    expert_ids = lax.broadcasted_iota(jnp.int32, (EXPERTS, TOK), 0)
    chosen = jnp.zeros((EXPERTS, TOK), f32)
    for k in range(routes_ref.shape[0]):
        chosen = chosen + jnp.where(routes_ref[k : k + 1, :] == expert_ids, 1.0, 0.0)
    before = lax.broadcasted_iota(jnp.int32, (TOK, TOK), 0)
    after = lax.broadcasted_iota(jnp.int32, (TOK, TOK), 1)
    upper = jnp.where(before <= after, 1.0, 0.0).astype(bf16)
    counted = jnp.dot(chosen.astype(bf16), upper, preferred_element_type=f32)
    position = jnp.where(chosen > 0.0, counted - 1.0, -1.0)
    pos_ref[...] = position
    slot_ids = lax.broadcasted_iota(jnp.int32, (SLOTS, TOK), 0).astype(f32)
    tokens = tokens_ref[...]
    group = 8
    for start in range(0, EXPERTS, group):
        picks = [
            jnp.where(slot_ids == position[e : e + 1, :], 1.0, 0.0)
            for e in range(start, start + group)
        ]
        pick = jnp.concatenate(picks, axis=0).astype(bf16)
        rows = jnp.dot(pick, tokens, preferred_element_type=f32)
        for i in range(group):
            out_ref[start + i] = rows[i * SLOTS : (i + 1) * SLOTS].astype(bf16)
    rest = weight_ref[...]
    logits = jnp.zeros((EXPERTS, TOK), f32)
    for _ in range(3):
        term = rest.astype(bf16)
        rest = rest - term.astype(f32)
        logits = logits + lax.dot_general(
            term, input_ref[...], (((1,), (1,)), ((), ())), preferred_element_type=f32
        )
    logit_ref[...] = logits


def pack(routes_t, tokens, router_input, weight_t):
    width = tokens.shape[1]
    return pl.pallas_call(
        pack_kernel,
        out_shape=(
            jax.ShapeDtypeStruct((EXPERTS, SLOTS, width), bf16),
            jax.ShapeDtypeStruct((EXPERTS, TOK), f32),
            jax.ShapeDtypeStruct((EXPERTS, TOK), f32),
        ),
        compiler_params=pltpu.CompilerParams(vmem_limit_bytes=VMEM_LIMIT),
        cost_estimate=pl.CostEstimate(flops=300_000_000, bytes_accessed=2_800_000, transcendentals=0),
    )(routes_t, tokens, router_input, weight_t)


def upstream_kernel(first_ref, rows_ref, down_ref, *refs):
    refs[-1][0] = lax.dot_general(
        rows_ref[...], down_ref[...], (((1,), (1,)), ((), ())), preferred_element_type=f32
    ).astype(bf16)


def upstream_partial(rows, down, place, core, after):
    count, width = rows.shape
    share = down.shape[0] // 8
    grid_spec = pltpu.PrefetchScalarGridSpec(
        num_scalar_prefetch=1,
        grid=(4,),
        in_specs=[
            pl.BlockSpec((count, width), lambda g, p: (0, 0)),
            pl.BlockSpec((share, width), lambda g, p: (2 * lax.rem(p[0] + g, 4) + p[1], 0)),
            pl.BlockSpec(memory_space=pl.ANY),
        ],
        out_specs=pl.BlockSpec((1, count, share), lambda g, p: (g, 0, 0)),
    )
    return pl.pallas_call(
        upstream_kernel,
        grid_spec=grid_spec,
        out_shape=jax.ShapeDtypeStruct((4, count, share), bf16),
        compiler_params=pltpu.CompilerParams(vmem_limit_bytes=VMEM_LIMIT),
        cost_estimate=pl.CostEstimate(
            flops=count * width * down.shape[0], bytes_accessed=6_300_000, transcendentals=0
        ),
    )(jnp.stack([place, core]), rows, down, after)


def back_kernel(hidden_ref, down_ref, out_ref):
    parts = hidden_ref.shape[0]
    whole = jnp.concatenate([hidden_ref[g] for g in range(parts)], axis=1)
    out_ref[...] = jnp.dot(whole, down_ref[...], preferred_element_type=f32)


def hidden_times_down(hidden, down):
    parts, count, share = hidden.shape
    width = down.shape[1]
    steps = 4
    block = count // steps
    return pl.pallas_call(
        back_kernel,
        grid=(steps,),
        in_specs=[
            pl.BlockSpec((parts, block, share), lambda g: (0, g, 0)),
            pl.BlockSpec((parts * share, width), lambda g: (0, 0)),
        ],
        out_specs=pl.BlockSpec((block, width), lambda g: (g, 0)),
        out_shape=jax.ShapeDtypeStruct((count, width), f32),
        compiler_params=pltpu.CompilerParams(vmem_limit_bytes=VMEM_LIMIT),
        cost_estimate=pl.CostEstimate(
            flops=2 * count * width * down.shape[0], bytes_accessed=12_500_000, transcendentals=0
        ),
    )(hidden, down)


def grad_down_kernel(hidden_ref, rows_ref, gate_ref, out_ref, scaled_ref):
    @pl.when(pl.program_id(0) == 0)
    def _():
        scaled_ref[...] = (gate_ref[...] * rows_ref[...].astype(f32)).astype(bf16)

    out_ref[0] = lax.dot_general(
        hidden_ref[0], scaled_ref[...], (((0,), (0,)), ((), ())), preferred_element_type=f32
    ).astype(bf16)


def grad_down_of(hidden, rows, gate):
    parts, count, share = hidden.shape
    width = rows.shape[1]
    return pl.pallas_call(
        grad_down_kernel,
        grid=(parts,),
        in_specs=[
            pl.BlockSpec((1, count, share), lambda g: (g, 0, 0)),
            pl.BlockSpec((count, width), lambda g: (0, 0)),
            pl.BlockSpec((count, 1), lambda g: (0, 0)),
        ],
        out_specs=pl.BlockSpec((1, share, width), lambda g: (0, g, 0)),
        out_shape=jax.ShapeDtypeStruct((1, parts * share, width), bf16),
        scratch_shapes=[pltpu.VMEM((count, width), bf16)],
        compiler_params=pltpu.CompilerParams(vmem_limit_bytes=VMEM_LIMIT),
        cost_estimate=pl.CostEstimate(
            flops=2 * count * width * parts * share, bytes_accessed=12_500_000, transcendentals=0
        ),
    )(hidden, rows, gate)


def exchange(value, axes):
    return lax.all_to_all(value, axes, split_axis=0, concat_axis=0, tiled=True)


def spread(value, axes, copies):
    return exchange(jnp.broadcast_to(value[None], (copies,) + value.shape), axes)


def swap(pieces, axes, size, stride=1):
    got = [pieces[0]]
    for k in range(1, size // stride):
        pairs = [(i, (i + k * stride) % size) for i in range(size)]
        got.append(lax.ppermute(pieces[k], axes, pairs))
    return got


def to_neighbour(value):
    return lax.ppermute(value, "z", [(i, i ^ 1) for i in range(8)])


def total_of(pieces):
    total = pieces[0].astype(f32)
    for piece in pieces[1:]:
        total = total + piece.astype(f32)
    return total


BLOCK = 40
PADDED = 8 * BLOCK
SHARE = LATENT // 8


def block_of(piece, z_at, sign):
    base = z_at + sign * 2 * (piece // 2)
    base = jnp.where(base >= 8, base - 8, jnp.where(base < 0, base + 8, base))
    other = jnp.where(base % 2 == 0, base + 1, base - 1)
    return jnp.where(piece % 2 == 0, base, other)


def cut_kernel(z_ref, total_ref, after_ref, *outs):
    row = lax.broadcasted_iota(jnp.int32, (PADDED, LATENT), 0)
    column = lax.broadcasted_iota(jnp.int32, (PADDED, LATENT), 1)
    piece = row // BLOCK
    within = row - piece * BLOCK
    block = block_of(piece, z_ref[0], 1)
    source = jnp.where(within < SHARE, block * SHARE + within, -1)
    pick = jnp.where(source == column, 1.0, 0.0).astype(bf16)
    rows = jnp.dot(pick, total_ref[...], preferred_element_type=f32)
    for k in range(4):
        outs[k][...] = rows[2 * k * BLOCK : 2 * (k + 1) * BLOCK].astype(bf16)


def gram_kernel(z_ref, *refs):
    parts, whole_ref, gram_ref = refs[:4], refs[6], refs[7]
    rows = jnp.concatenate([part[...].astype(f32) for part in parts], axis=0).astype(bf16)
    row = lax.broadcasted_iota(jnp.int32, (LATENT, PADDED), 0)
    column = lax.broadcasted_iota(jnp.int32, (LATENT, PADDED), 1)
    piece = column // BLOCK
    within = column - piece * BLOCK
    block = block_of(piece, z_ref[0], -1)
    target = jnp.where(within < SHARE, block * SHARE + within, -1)
    pick = jnp.where(target == row, 1.0, 0.0).astype(bf16)
    whole = jnp.dot(pick, rows, preferred_element_type=f32).astype(bf16)
    whole_ref[...] = whole
    gram_ref[...] = lax.dot_general(
        whole, whole, (((1,), (1,)), ((), ())), preferred_element_type=f32
    )


def newton_kernel(grams_ref, whole_ref, after_ref, out_ref):
    gram = total_of([grams_ref[g] for g in range(grams_ref.shape[0])])
    row = lax.broadcasted_iota(jnp.int32, (LATENT, LATENT), 0)
    column = lax.broadcasted_iota(jnp.int32, (LATENT, LATENT), 1)
    eye = jnp.where(row == column, 1.0, 0.0)
    squares = jnp.sum(jnp.sum(gram * eye, axis=1, keepdims=True), axis=0, keepdims=True)
    inverse = 1.0 / (jnp.sqrt(squares) + NORM_EPS)
    dot = lambda a, b: jnp.dot(
        a, b, precision=lax.Precision.HIGHEST, preferred_element_type=f32
    )
    first = gram * inverse * inverse
    poly_first = COEF_A * eye + COEF_B * first + COEF_C * dot(first, first)
    second = dot(poly_first, dot(first, poly_first))
    poly_second = COEF_A * eye + COEF_B * second + COEF_C * dot(second, second)
    factor = 0.2 * float(D) ** 0.5
    both = dot(poly_second, poly_first) * (factor * inverse)
    high = both.astype(bf16)
    low = (both - high.astype(f32)).astype(bf16)
    whole = whole_ref[...]
    out_ref[...] = (
        jnp.dot(high, whole, preferred_element_type=f32)
        + jnp.dot(low, whole, preferred_element_type=f32)
    ).astype(bf16)


SMEM = pl.BlockSpec(memory_space=pltpu.SMEM)
WHOLE = pl.BlockSpec(memory_space=pltpu.VMEM)


PAIR = jax.ShapeDtypeStruct((2 * BLOCK, D // 8), bf16)
AFTER = pl.BlockSpec(memory_space=pl.ANY)
PARAMS = pltpu.CompilerParams(vmem_limit_bytes=VMEM_LIMIT)


def muon_blocks(attention, after):
    part = lax.psum_scatter(attention, "y", scatter_dimension=0, tiled=True)[0]
    return pl.pallas_call(
        cut_kernel,
        in_specs=[SMEM, WHOLE, AFTER],
        out_specs=[WHOLE] * 4,
        out_shape=[PAIR] * 4,
        compiler_params=PARAMS,
        cost_estimate=pl.CostEstimate(flops=170_000_000, bytes_accessed=1_200_000, transcendentals=0),
    )(lax.axis_index("z")[None], part, after)


def muon_gram(row_block, first, second):
    pair = jnp.concatenate([row_block, to_neighbour(row_block)], axis=0)
    gathered = swap([pair] * 4, "z", 8, 2)
    return pl.pallas_call(
        gram_kernel,
        in_specs=[SMEM] + [WHOLE] * 4 + [AFTER] * 2,
        out_specs=[WHOLE] * 2,
        out_shape=[
            jax.ShapeDtypeStruct((LATENT, D // 8), bf16),
            jax.ShapeDtypeStruct((LATENT, LATENT), f32),
        ],
        compiler_params=PARAMS,
        cost_estimate=pl.CostEstimate(flops=300_000_000, bytes_accessed=1_600_000, transcendentals=0),
    )(lax.axis_index("z")[None], *gathered, first, second)


def muon_update_of(whole, grams, after):
    return pl.pallas_call(
        newton_kernel,
        in_specs=[WHOLE, WHOLE, AFTER],
        out_specs=WHOLE,
        out_shape=jax.ShapeDtypeStruct((LATENT, D // 8), bf16),
        compiler_params=PARAMS,
        cost_estimate=pl.CostEstimate(
            flops=3_000_000_000, bytes_accessed=3_600_000, transcendentals=0
        ),
    )(grams, whole, after)


def muon_spread(update):
    y_at = lax.axis_index("y")
    out = jnp.zeros((4,) + update.shape, bf16)
    for k, got in enumerate(swap([update] * 4, "y", 4)):
        out = lax.dynamic_update_index_in_dim(out, got, lax.rem(y_at + 4 - k, 4), 0)
    return out


def join_kernel(first_ref, second_ref, after_ref, out_ref):
    out_ref[:, 0, :] = first_ref[...]
    out_ref[:, 1, :] = second_ref[...]


def join(first, second, after):
    return pl.pallas_call(
        join_kernel,
        in_specs=[WHOLE, WHOLE, AFTER],
        out_specs=WHOLE,
        out_shape=jax.ShapeDtypeStruct((first.shape[0], 2, first.shape[1]), f32),
        compiler_params=PARAMS,
    )(first, second, after)


def hand_kernel(value_ref, *refs):
    refs[-1][...] = value_ref[...]


def hand(value, *after):
    return pl.pallas_call(
        hand_kernel,
        in_specs=[WHOLE] + [AFTER] * len(after),
        out_specs=WHOLE,
        out_shape=jax.ShapeDtypeStruct(value.shape, value.dtype),
        compiler_params=PARAMS,
    )(value, *after)


def add_kernel(values_ref, *refs):
    total = values_ref[0]
    for i in range(1, values_ref.shape[0]):
        total = total + values_ref[i]
    refs[-1][...] = total


def add_up(values, *after):
    return pl.pallas_call(
        add_kernel,
        in_specs=[WHOLE] + [AFTER] * len(after),
        out_specs=WHOLE,
        out_shape=jax.ShapeDtypeStruct(values.shape[1:], values.dtype),
        compiler_params=PARAMS,
    )(values, *after)


def on_device(
    out_grad,
    router_input,
    router_weight,
    routes,
    balance_grad,
    saved_hidden,
    expert_down,
    attention_grads,
):
    width = out_grad.shape[1]
    down = expert_down[0]
    share = saved_hidden.shape[3]
    count = CAP * EXPERTS
    weight_t = router_weight.T
    input_f = router_input.astype(f32)
    packed, position, partial_logits = pack(routes.T, out_grad, router_input, weight_t)
    rows_got = exchange(packed, EP)
    hidden_share = jnp.swapaxes(saved_hidden[0], 0, 1).reshape(count, share)
    hidden = lax.all_gather(hidden_share, FS, axis=0, tiled=False)
    logits = total_of(swap([partial_logits] * 8, FS, 8))

    scores = jax.nn.sigmoid(logits)
    chosen = position >= 0.0
    selected = chosen.astype(f32)
    score_total = jnp.sum(selected * scores, axis=0, keepdims=True)
    gates = (selected * ROUTE_SCALE * scores / score_total).astype(bf16).astype(f32)
    slot_ids = jnp.arange(SLOTS, dtype=jnp.int32).astype(f32)
    matches = position[:, None, :] == slot_ids[None, :, None]
    slot_gates = jnp.sum(jnp.where(matches, gates[:, None, :], 0.0), axis=2)
    back = hidden_times_down(hidden, down)
    blocks = muon_blocks(attention_grads[0], slot_gates)
    pair_sum = total_of(swap(blocks, "z", 8, 2))
    for_next = to_neighbour(pair_sum[BLOCK:].astype(bf16))
    row_block = (pair_sum[:BLOCK] + for_next.astype(f32)).astype(bf16)
    ready = (blocks[0][0, 0] < f32(jnp.inf)) & (back[0, 0] < f32(jnp.inf))
    keep = jnp.where(ready, 1.0, 0.0).astype(bf16)
    rows = jnp.swapaxes(rows_got[:, :CAP] * keep, 0, 1).reshape(count, width)
    gate_part = jnp.sum(back * rows.astype(f32), axis=1)
    gate_part_t = jnp.pad(gate_part.reshape(CAP, EXPERTS).T, ((0, 0), (0, SLOTS - CAP)))
    joined = join(slot_gates, gate_part_t, position)
    both_got = exchange(joined, EP)
    gate_column = both_got[:, 0, :CAP].T.reshape(count, 1)
    returned = both_got[:, 1]
    back_part = jnp.sum(jnp.where(matches, returned[:, :, None], 0.0), axis=1)
    grad_down = grad_down_of(hidden, rows, gate_column)
    x_at, core_at = lax.axis_index("x"), lax.axis_index("c")
    for_other = upstream_partial(rows, down, x_at, 1 - core_at, joined)
    from_other = lax.ppermute(for_other, "c", [(0, 1), (1, 0)])
    for_own = upstream_partial(rows, down, x_at, core_at, for_other)
    whole, gram = muon_gram(row_block, both_got, for_own)
    grams = lax.all_gather(gram, FS, axis=0, tiled=False)
    both_cores = (from_other.astype(f32) + for_own.astype(f32)).astype(bf16)
    upstream = total_of(swap([both_cores[k] for k in range(4)], "x", 4))
    back_parts = spread(hand(back_part, gram), FS, 8)
    gate_back = add_up(back_parts, grad_down)

    grad_hidden = (gate_column * upstream).astype(bf16)
    grad_hidden = jnp.swapaxes(grad_hidden.reshape(CAP, EXPERTS, share), 0, 1)[None]

    weighted = jnp.sum(selected * gate_back * scores, axis=0, keepdims=True) / score_total
    score_grad = balance_grad.T + selected * (ROUTE_SCALE / score_total) * (gate_back - weighted)
    logit_grad = score_grad * scores * (1.0 - scores)
    router_part = jnp.dot(logit_grad, input_f, precision=lax.Precision.HIGHEST)
    router_got = exchange(router_part.reshape(EXPERTS, 1, width), EP)
    update = muon_update_of(whole, grams, router_part)
    muon_update = muon_spread(update)
    router_row = add_up(router_got, update)
    router_grad = spread(router_row, EP, EXPERTS).reshape(EXPERTS, width).T
    token_grad = lax.dot_general(
        logit_grad, weight_t, (((0,), (0,)), ((), ())), precision=lax.Precision.HIGHEST
    ).astype(bf16)
    return (grad_hidden, grad_down, router_grad, token_grad, muon_update)


def solution(mesh):
    split = Mesh(mesh.devices.reshape(4, 2, 8, 4), ("x", "c", "z", "y"))
    in_specs = (
        P(EP, FS),
        P(EP, FS),
        P(FS, None),
        P(EP, None),
        P(EP, None),
        P(EP, None, None, FS),
        P(EP, None, FS),
        P(EP, None, None, FS),
    )
    out_specs = (
        P(EP, None, None, FS),
        P(EP, None, FS),
        P(FS, None),
        P(EP, FS),
        P(None, None, FS),
    )
    return jax.shard_map(
        on_device, mesh=split, in_specs=in_specs, out_specs=out_specs, check_vma=False
    )
```

```python
import jax
import jax.numpy as jnp
from jax import lax
from jax.experimental import pallas as pl
from jax.experimental.pallas import tpu as pltpu
from jax.sharding import Mesh, PartitionSpec as P

D = 7168
LATENT = 288
ROUTE_SCALE = 2.827
NORM_EPS = 1e-07
COEF_A = 3.4445
COEF_B = -4.775
COEF_C = 2.0315
CAP = 36
SLOTS = 40
EXPERTS = 32
TOK = 128

FS = ("x", "c")
EP = ("z", "y")
f32 = jnp.float32
bf16 = jnp.bfloat16
VMEM_LIMIT = 48 * 1024 * 1024


def pack_kernel(routes_ref, tokens_ref, input_ref, weight_ref, out_ref, pos_ref, logit_ref):
    expert_ids = lax.broadcasted_iota(jnp.int32, (EXPERTS, TOK), 0)
    chosen = jnp.zeros((EXPERTS, TOK), f32)
    for k in range(routes_ref.shape[0]):
        chosen = chosen + jnp.where(routes_ref[k : k + 1, :] == expert_ids, 1.0, 0.0)
    before = lax.broadcasted_iota(jnp.int32, (TOK, TOK), 0)
    after = lax.broadcasted_iota(jnp.int32, (TOK, TOK), 1)
    upper = jnp.where(before <= after, 1.0, 0.0).astype(bf16)
    counted = jnp.dot(chosen.astype(bf16), upper, preferred_element_type=f32)
    position = jnp.where(chosen > 0.0, counted - 1.0, -1.0)
    pos_ref[...] = position
    slot_ids = lax.broadcasted_iota(jnp.int32, (SLOTS, TOK), 0).astype(f32)
    tokens = tokens_ref[...]
    group = 8
    for start in range(0, EXPERTS, group):
        picks = [
            jnp.where(slot_ids == position[e : e + 1, :], 1.0, 0.0)
            for e in range(start, start + group)
        ]
        pick = jnp.concatenate(picks, axis=0).astype(bf16)
        rows = jnp.dot(pick, tokens, preferred_element_type=f32)
        for i in range(group):
            out_ref[start + i] = rows[i * SLOTS : (i + 1) * SLOTS].astype(bf16)
    rest = weight_ref[...]
    logits = jnp.zeros((EXPERTS, TOK), f32)
    for _ in range(3):
        term = rest.astype(bf16)
        rest = rest - term.astype(f32)
        logits = logits + lax.dot_general(
            term, input_ref[...], (((1,), (1,)), ((), ())), preferred_element_type=f32
        )
    logit_ref[...] = logits


def pack(routes_t, tokens, router_input, weight_t):
    width = tokens.shape[1]
    return pl.pallas_call(
        pack_kernel,
        out_shape=(
            jax.ShapeDtypeStruct((EXPERTS, SLOTS, width), bf16),
            jax.ShapeDtypeStruct((EXPERTS, TOK), f32),
            jax.ShapeDtypeStruct((EXPERTS, TOK), f32),
        ),
        compiler_params=pltpu.CompilerParams(vmem_limit_bytes=VMEM_LIMIT),
        cost_estimate=pl.CostEstimate(flops=300_000_000, bytes_accessed=2_800_000, transcendentals=0),
    )(routes_t, tokens, router_input, weight_t)


def upstream_kernel(first_ref, rows_ref, down_ref, *refs):
    refs[-1][0] = lax.dot_general(
        rows_ref[...], down_ref[...], (((1,), (1,)), ((), ())), preferred_element_type=f32
    ).astype(bf16)


def upstream_partial(rows, down, place, core, after):
    count, width = rows.shape
    share = down.shape[0] // 8
    grid_spec = pltpu.PrefetchScalarGridSpec(
        num_scalar_prefetch=1,
        grid=(4,),
        in_specs=[
            pl.BlockSpec((count, width), lambda g, p: (0, 0)),
            pl.BlockSpec((share, width), lambda g, p: (2 * lax.rem(p[0] + g, 4) + p[1], 0)),
            pl.BlockSpec(memory_space=pl.ANY),
        ],
        out_specs=pl.BlockSpec((1, count, share), lambda g, p: (g, 0, 0)),
    )
    return pl.pallas_call(
        upstream_kernel,
        grid_spec=grid_spec,
        out_shape=jax.ShapeDtypeStruct((4, count, share), bf16),
        compiler_params=pltpu.CompilerParams(vmem_limit_bytes=VMEM_LIMIT),
        cost_estimate=pl.CostEstimate(
            flops=count * width * down.shape[0], bytes_accessed=6_300_000, transcendentals=0
        ),
    )(jnp.stack([place, core]), rows, down, after)


def back_kernel(hidden_ref, down_ref, out_ref):
    parts = hidden_ref.shape[0]
    whole = jnp.concatenate([hidden_ref[g] for g in range(parts)], axis=1)
    out_ref[...] = jnp.dot(whole, down_ref[...], preferred_element_type=f32)


def hidden_times_down(hidden, down):
    parts, count, share = hidden.shape
    width = down.shape[1]
    steps = 4
    block = count // steps
    return pl.pallas_call(
        back_kernel,
        grid=(steps,),
        in_specs=[
            pl.BlockSpec((parts, block, share), lambda g: (0, g, 0)),
            pl.BlockSpec((parts * share, width), lambda g: (0, 0)),
        ],
        out_specs=pl.BlockSpec((block, width), lambda g: (g, 0)),
        out_shape=jax.ShapeDtypeStruct((count, width), f32),
        compiler_params=pltpu.CompilerParams(vmem_limit_bytes=VMEM_LIMIT),
        cost_estimate=pl.CostEstimate(
            flops=2 * count * width * down.shape[0], bytes_accessed=12_500_000, transcendentals=0
        ),
    )(hidden, down)


def grad_down_kernel(hidden_ref, rows_ref, gate_ref, out_ref, scaled_ref):
    @pl.when(pl.program_id(0) == 0)
    def _():
        scaled_ref[...] = (gate_ref[...] * rows_ref[...].astype(f32)).astype(bf16)

    out_ref[0] = lax.dot_general(
        hidden_ref[0], scaled_ref[...], (((0,), (0,)), ((), ())), preferred_element_type=f32
    ).astype(bf16)


def grad_down_of(hidden, rows, gate):
    parts, count, share = hidden.shape
    width = rows.shape[1]
    return pl.pallas_call(
        grad_down_kernel,
        grid=(parts,),
        in_specs=[
            pl.BlockSpec((1, count, share), lambda g: (g, 0, 0)),
            pl.BlockSpec((count, width), lambda g: (0, 0)),
            pl.BlockSpec((count, 1), lambda g: (0, 0)),
        ],
        out_specs=pl.BlockSpec((1, share, width), lambda g: (0, g, 0)),
        out_shape=jax.ShapeDtypeStruct((1, parts * share, width), bf16),
        scratch_shapes=[pltpu.VMEM((count, width), bf16)],
        compiler_params=pltpu.CompilerParams(vmem_limit_bytes=VMEM_LIMIT),
        cost_estimate=pl.CostEstimate(
            flops=2 * count * width * parts * share, bytes_accessed=12_500_000, transcendentals=0
        ),
    )(hidden, rows, gate)


def exchange(value, axes):
    return lax.all_to_all(value, axes, split_axis=0, concat_axis=0, tiled=True)


def spread(value, axes, copies):
    return exchange(jnp.broadcast_to(value[None], (copies,) + value.shape), axes)


def swap(pieces, axes, size):
    got = [pieces[0]]
    for k in range(1, size):
        got.append(lax.ppermute(pieces[k], axes, [(i, (i + k) % size) for i in range(size)]))
    return got


def total_of(pieces):
    total = pieces[0].astype(f32)
    for piece in pieces[1:]:
        total = total + piece.astype(f32)
    return total


BLOCK = 40
PADDED = 8 * BLOCK
SHARE = LATENT // 8
HALF = LATENT // 2


def cut_kernel(y_ref, half_ref, after_ref, *outs):
    row = lax.broadcasted_iota(jnp.int32, (4 * BLOCK, HALF), 0)
    column = lax.broadcasted_iota(jnp.int32, (4 * BLOCK, HALF), 1)
    piece = row // BLOCK
    within = row - piece * BLOCK
    block = (piece + y_ref[0]) % 4
    source = jnp.where(within < SHARE, block * SHARE + within, -1)
    pick = jnp.where(source == column, 1.0, 0.0).astype(bf16)
    rows = jnp.dot(pick, half_ref[...], preferred_element_type=f32)
    for k in range(4):
        outs[k][...] = rows[k * BLOCK : (k + 1) * BLOCK].astype(bf16)


def gram_kernel(place_ref, *refs):
    parts, whole_ref, gram_ref = refs[:4], refs[5], refs[6]
    rows = jnp.concatenate([part[...].astype(f32) for part in parts], axis=0).astype(bf16)
    row = lax.broadcasted_iota(jnp.int32, (LATENT, PADDED), 0)
    column = lax.broadcasted_iota(jnp.int32, (LATENT, PADDED), 1)
    piece = column // BLOCK
    within = column - piece * BLOCK
    block = (place_ref[0] + 4 - piece // 2) % 4
    half = (place_ref[1] + piece) % 2
    target = jnp.where(within < SHARE, half * HALF + block * SHARE + within, -1)
    pick = jnp.where(target == row, 1.0, 0.0).astype(bf16)
    whole = jnp.dot(pick, rows, preferred_element_type=f32).astype(bf16)
    whole_ref[...] = whole
    gram_ref[...] = lax.dot_general(
        whole, whole, (((1,), (1,)), ((), ())), preferred_element_type=f32
    )


def newton_kernel(half_ref, grams_ref, whole_ref, after_ref, out_ref, scratch):
    gram = total_of([grams_ref[g] for g in range(grams_ref.shape[0])])
    row = lax.broadcasted_iota(jnp.int32, (LATENT, LATENT), 0)
    column = lax.broadcasted_iota(jnp.int32, (LATENT, LATENT), 1)
    eye = jnp.where(row == column, 1.0, 0.0)
    squares = jnp.sum(jnp.sum(gram * eye, axis=1, keepdims=True), axis=0, keepdims=True)
    inverse = 1.0 / (jnp.sqrt(squares) + NORM_EPS)
    dot = lambda a, b: jnp.dot(
        a, b, precision=lax.Precision.HIGHEST, preferred_element_type=f32
    )
    first = gram * inverse * inverse
    poly_first = COEF_A * eye + COEF_B * first + COEF_C * dot(first, first)
    second = dot(poly_first, dot(first, poly_first))
    poly_second = COEF_A * eye + COEF_B * second + COEF_C * dot(second, second)
    factor = 0.2 * float(D) ** 0.5
    scratch[...] = dot(poly_second, poly_first) * (factor * inverse)
    both = scratch[pl.ds(pl.multiple_of(half_ref[0] * HALF, 8), HALF), :]
    high = both.astype(bf16)
    low = (both - high.astype(f32)).astype(bf16)
    whole = whole_ref[...]
    out_ref[...] = (
        jnp.dot(high, whole, preferred_element_type=f32)
        + jnp.dot(low, whole, preferred_element_type=f32)
    ).astype(bf16)


SMEM = pl.BlockSpec(memory_space=pltpu.SMEM)
WHOLE = pl.BlockSpec(memory_space=pltpu.VMEM)


PIECE = jax.ShapeDtypeStruct((BLOCK, D // 8), bf16)
AFTER = pl.BlockSpec(memory_space=pl.ANY)
PARAMS = pltpu.CompilerParams(vmem_limit_bytes=VMEM_LIMIT)


def muon_pair(attention, after):
    mats, latent, width = attention.shape
    half = lax.psum_scatter(
        attention.reshape(mats * latent, width), "z", scatter_dimension=0, tiled=True
    )
    blocks = pl.pallas_call(
        cut_kernel,
        in_specs=[SMEM, WHOLE, AFTER],
        out_specs=[WHOLE] * 4,
        out_shape=[PIECE] * 4,
        compiler_params=PARAMS,
        cost_estimate=pl.CostEstimate(flops=50_000_000, bytes_accessed=600_000, transcendentals=0),
    )(lax.axis_index("y")[None], half, after)
    block = total_of(swap(blocks, "y", 4)).astype(bf16)
    other = lax.ppermute(block, "z", [(i, i ^ 1) for i in range(8)])
    return jnp.concatenate([block, other], axis=0)


def muon_gram(pair, after):
    gathered = swap([pair] * 4, "y", 4)
    place = jnp.stack([lax.axis_index("y"), lax.rem(lax.axis_index("z"), 2)])
    return pl.pallas_call(
        gram_kernel,
        in_specs=[SMEM] + [WHOLE] * 4 + [AFTER],
        out_specs=[WHOLE] * 2,
        out_shape=[
            jax.ShapeDtypeStruct((LATENT, D // 8), bf16),
            jax.ShapeDtypeStruct((LATENT, LATENT), f32),
        ],
        compiler_params=PARAMS,
        cost_estimate=pl.CostEstimate(flops=300_000_000, bytes_accessed=1_600_000, transcendentals=0),
    )(place, *gathered, after)


def muon_update_of(whole, grams, after):
    return pl.pallas_call(
        newton_kernel,
        in_specs=[SMEM, WHOLE, WHOLE, AFTER],
        out_specs=WHOLE,
        out_shape=jax.ShapeDtypeStruct((HALF, D // 8), bf16),
        scratch_shapes=[pltpu.VMEM((LATENT, LATENT), f32)],
        compiler_params=PARAMS,
        cost_estimate=pl.CostEstimate(
            flops=3_000_000_000, bytes_accessed=3_600_000, transcendentals=0
        ),
    )(lax.rem(lax.axis_index("z"), 2)[None], grams, whole, after)


def join_kernel(first_ref, second_ref, after_ref, out_ref):
    out_ref[:, 0, :] = first_ref[...]
    out_ref[:, 1, :] = second_ref[...]


def join(first, second, after):
    return pl.pallas_call(
        join_kernel,
        in_specs=[WHOLE, WHOLE, AFTER],
        out_specs=WHOLE,
        out_shape=jax.ShapeDtypeStruct((first.shape[0], 2, first.shape[1]), f32),
        compiler_params=PARAMS,
    )(first, second, after)


def hand_kernel(value_ref, *refs):
    refs[-1][...] = value_ref[...]


def hand(value, *after):
    return pl.pallas_call(
        hand_kernel,
        in_specs=[WHOLE] + [AFTER] * len(after),
        out_specs=WHOLE,
        out_shape=jax.ShapeDtypeStruct(value.shape, value.dtype),
        compiler_params=PARAMS,
    )(value, *after)


def add_kernel(values_ref, *refs):
    total = values_ref[0]
    for i in range(1, values_ref.shape[0]):
        total = total + values_ref[i]
    refs[-1][...] = total


def add_up(values, *after):
    return pl.pallas_call(
        add_kernel,
        in_specs=[WHOLE] + [AFTER] * len(after),
        out_specs=WHOLE,
        out_shape=jax.ShapeDtypeStruct(values.shape[1:], values.dtype),
        compiler_params=PARAMS,
    )(values, *after)


def on_device(
    out_grad,
    router_input,
    router_weight,
    routes,
    balance_grad,
    saved_hidden,
    expert_down,
    attention_grads,
):
    width = out_grad.shape[1]
    down = expert_down[0]
    share = saved_hidden.shape[3]
    count = CAP * EXPERTS
    weight_t = router_weight.T
    input_f = router_input.astype(f32)
    packed, position, partial_logits = pack(routes.T, out_grad, router_input, weight_t)
    rows_got = exchange(packed, EP)
    hidden_share = jnp.swapaxes(saved_hidden[0], 0, 1).reshape(count, share)
    hidden = lax.all_gather(hidden_share, FS, axis=0, tiled=False)
    logits = total_of(swap([partial_logits] * 8, FS, 8))

    scores = jax.nn.sigmoid(logits)
    chosen = position >= 0.0
    selected = chosen.astype(f32)
    score_total = jnp.sum(selected * scores, axis=0, keepdims=True)
    gates = (selected * ROUTE_SCALE * scores / score_total).astype(bf16).astype(f32)
    slot_ids = jnp.arange(SLOTS, dtype=jnp.int32).astype(f32)
    matches = position[:, None, :] == slot_ids[None, :, None]
    slot_gates = jnp.sum(jnp.where(matches, gates[:, None, :], 0.0), axis=2)
    back = hidden_times_down(hidden, down)
    pair = muon_pair(attention_grads[0], slot_gates)
    whole, gram = muon_gram(pair, back)
    grams = lax.all_gather(gram, FS, axis=0, tiled=False)
    ready = (pair[0, 0] < f32(jnp.inf)) & (back[0, 0] < f32(jnp.inf))
    keep = jnp.where(ready, 1.0, 0.0).astype(bf16)
    rows = jnp.swapaxes(rows_got[:, :CAP] * keep, 0, 1).reshape(count, width)
    gate_part = jnp.sum(back * rows.astype(f32), axis=1)
    gate_part_t = jnp.pad(gate_part.reshape(CAP, EXPERTS).T, ((0, 0), (0, SLOTS - CAP)))
    joined = join(slot_gates, gate_part_t, position)
    both_got = exchange(joined, EP)
    gate_column = both_got[:, 0, :CAP].T.reshape(count, 1)
    returned = both_got[:, 1]
    back_part = jnp.sum(jnp.where(matches, returned[:, :, None], 0.0), axis=1)
    grad_down = grad_down_of(hidden, rows, gate_column)
    x_at, core_at = lax.axis_index("x"), lax.axis_index("c")
    for_other = upstream_partial(rows, down, x_at, 1 - core_at, joined)
    from_other = lax.ppermute(for_other, "c", [(0, 1), (1, 0)])
    for_own = upstream_partial(rows, down, x_at, core_at, for_other)
    both_cores = (from_other.astype(f32) + for_own.astype(f32)).astype(bf16)
    upstream = total_of(swap([both_cores[k] for k in range(4)], "x", 4))
    back_parts = spread(hand(back_part, for_own), FS, 8)
    gate_back = add_up(back_parts, grad_down)

    grad_hidden = (gate_column * upstream).astype(bf16)
    grad_hidden = jnp.swapaxes(grad_hidden.reshape(CAP, EXPERTS, share), 0, 1)[None]

    weighted = jnp.sum(selected * gate_back * scores, axis=0, keepdims=True) / score_total
    score_grad = balance_grad.T + selected * (ROUTE_SCALE / score_total) * (gate_back - weighted)
    logit_grad = score_grad * scores * (1.0 - scores)
    router_part = jnp.dot(logit_grad, input_f, precision=lax.Precision.HIGHEST)
    router_got = exchange(router_part.reshape(EXPERTS, 1, width), EP)
    update = muon_update_of(whole, grams, router_part)
    muon_update = lax.all_gather(update, "z", axis=0, tiled=True).reshape(4, LATENT, width)
    router_row = add_up(router_got, update)
    router_grad = spread(router_row, EP, EXPERTS).reshape(EXPERTS, width).T
    token_grad = lax.dot_general(
        logit_grad, weight_t, (((0,), (0,)), ((), ())), precision=lax.Precision.HIGHEST
    ).astype(bf16)
    return (grad_hidden, grad_down, router_grad, token_grad, muon_update)


def solution(mesh):
    split = Mesh(mesh.devices.reshape(4, 2, 8, 4), ("x", "c", "z", "y"))
    in_specs = (
        P(EP, FS),
        P(EP, FS),
        P(FS, None),
        P(EP, None),
        P(EP, None),
        P(EP, None, None, FS),
        P(EP, None, FS),
        P(EP, None, None, FS),
    )
    out_specs = (
        P(EP, None, None, FS),
        P(EP, None, FS),
        P(FS, None),
        P(EP, FS),
        P(None, None, FS),
    )
    return jax.shard_map(
        on_device, mesh=split, in_specs=in_specs, out_specs=out_specs, check_vma=False
    )
```

```python
import jax
import jax.numpy as jnp
from jax import lax
from jax.experimental import pallas as pl
from jax.experimental.pallas import tpu as pltpu
from jax.sharding import Mesh, PartitionSpec as P

D = 7168
LATENT = 288
ROUTE_SCALE = 2.827
NORM_EPS = 1e-07
COEF_A = 3.4445
COEF_B = -4.775
COEF_C = 2.0315
CAP = 36
SLOTS = 40
EXPERTS = 32
TOK = 128

FS = ("x", "c")
EP = ("z", "y")
f32 = jnp.float32
bf16 = jnp.bfloat16
VMEM_LIMIT = 48 * 1024 * 1024


def place_kernel(routes_ref, input_ref, weight_ref, pos_ref, logit_ref):
    expert_ids = lax.broadcasted_iota(jnp.int32, (EXPERTS, TOK), 0)
    chosen = jnp.zeros((EXPERTS, TOK), f32)
    for k in range(routes_ref.shape[0]):
        chosen = chosen + jnp.where(routes_ref[k : k + 1, :] == expert_ids, 1.0, 0.0)
    pos_ref[...] = slots_of(chosen)
    rest = weight_ref[...]
    logits = jnp.zeros((EXPERTS, TOK), f32)
    for _ in range(3):
        term = rest.astype(bf16)
        rest = rest - term.astype(f32)
        logits = logits + lax.dot_general(
            term, input_ref[...], (((1,), (1,)), ((), ())), preferred_element_type=f32
        )
    logit_ref[...] = logits


def slots_of(chosen):
    before = lax.broadcasted_iota(jnp.int32, (TOK, TOK), 0)
    after = lax.broadcasted_iota(jnp.int32, (TOK, TOK), 1)
    upper = jnp.where(before <= after, 1.0, 0.0).astype(bf16)
    counted = jnp.dot(chosen.astype(bf16), upper, preferred_element_type=f32)
    return jnp.where(chosen > 0.0, counted - 1.0, -1.0)


def place(routes_t, router_input, weight_t):
    return pl.pallas_call(
        place_kernel,
        out_shape=(
            jax.ShapeDtypeStruct((EXPERTS, TOK), f32),
            jax.ShapeDtypeStruct((EXPERTS, TOK), f32),
        ),
        compiler_params=pltpu.CompilerParams(vmem_limit_bytes=VMEM_LIMIT),
        cost_estimate=pl.CostEstimate(flops=30_000_000, bytes_accessed=400_000, transcendentals=0),
    )(routes_t, router_input, weight_t)


def pack_kernel(z_ref, blocks_ref, out_ref):
    expert = lax.broadcasted_iota(jnp.int32, (4, TOK), 0) + 4 * z_ref[0]
    expert = expert.astype(f32)
    picked = []
    for s in range(8):
        routes = blocks_ref[s, TOK:, :TOK].astype(f32)
        chosen = jnp.zeros((4, TOK), f32)
        for k in range(8):
            chosen = chosen + jnp.where(routes[k : k + 1, :] == expert, 1.0, 0.0)
        picked.append(chosen)
    position = slots_of(jnp.concatenate(picked, axis=0))
    slot_ids = lax.broadcasted_iota(jnp.int32, (SLOTS, TOK), 0).astype(f32)
    for s in range(8):
        picks = [
            jnp.where(slot_ids == position[4 * s + y : 4 * s + y + 1, :], 1.0, 0.0)
            for y in range(4)
        ]
        pick = jnp.concatenate(picks, axis=0).astype(bf16)
        rows = jnp.dot(pick, blocks_ref[s, :TOK, :], preferred_element_type=f32)
        for y in range(4):
            out_ref[y, s] = rows[y * SLOTS : (y + 1) * SLOTS].astype(bf16)


def pack(blocks, z_at):
    width = blocks.shape[2]
    return pl.pallas_call(
        pack_kernel,
        in_specs=[pl.BlockSpec(memory_space=pltpu.SMEM), pl.BlockSpec(memory_space=pltpu.VMEM)],
        out_specs=pl.BlockSpec(memory_space=pltpu.VMEM),
        out_shape=jax.ShapeDtypeStruct((4, 8, SLOTS, width), bf16),
        compiler_params=pltpu.CompilerParams(vmem_limit_bytes=VMEM_LIMIT),
        cost_estimate=pl.CostEstimate(flops=300_000_000, bytes_accessed=4_500_000, transcendentals=0),
    )(z_at[None], blocks)


def upstream_kernel(first_ref, rows_ref, down_ref, *refs):
    refs[-1][0] = lax.dot_general(
        rows_ref[...], down_ref[...], (((1,), (1,)), ((), ())), preferred_element_type=f32
    ).astype(bf16)


def upstream_partial(rows, down, place, core, after):
    count, width = rows.shape
    share = down.shape[0] // 8
    grid_spec = pltpu.PrefetchScalarGridSpec(
        num_scalar_prefetch=1,
        grid=(4,),
        in_specs=[
            pl.BlockSpec((count, width), lambda g, p: (0, 0)),
            pl.BlockSpec((share, width), lambda g, p: (2 * lax.rem(p[0] + g, 4) + p[1], 0)),
            pl.BlockSpec(memory_space=pl.ANY),
        ],
        out_specs=pl.BlockSpec((1, count, share), lambda g, p: (g, 0, 0)),
    )
    return pl.pallas_call(
        upstream_kernel,
        grid_spec=grid_spec,
        out_shape=jax.ShapeDtypeStruct((4, count, share), bf16),
        compiler_params=pltpu.CompilerParams(vmem_limit_bytes=VMEM_LIMIT),
        cost_estimate=pl.CostEstimate(
            flops=count * width * down.shape[0], bytes_accessed=6_300_000, transcendentals=0
        ),
    )(jnp.stack([place, core]), rows, down, after)


def back_kernel(hidden_ref, down_ref, out_ref):
    parts = hidden_ref.shape[0]
    whole = jnp.concatenate([hidden_ref[g] for g in range(parts)], axis=1)
    out_ref[...] = jnp.dot(whole, down_ref[...], preferred_element_type=f32)


def hidden_times_down(hidden, down):
    parts, count, share = hidden.shape
    width = down.shape[1]
    steps = 4
    block = count // steps
    return pl.pallas_call(
        back_kernel,
        grid=(steps,),
        in_specs=[
            pl.BlockSpec((parts, block, share), lambda g: (0, g, 0)),
            pl.BlockSpec((parts * share, width), lambda g: (0, 0)),
        ],
        out_specs=pl.BlockSpec((block, width), lambda g: (g, 0)),
        out_shape=jax.ShapeDtypeStruct((count, width), f32),
        compiler_params=pltpu.CompilerParams(vmem_limit_bytes=VMEM_LIMIT),
        cost_estimate=pl.CostEstimate(
            flops=2 * count * width * down.shape[0], bytes_accessed=12_500_000, transcendentals=0
        ),
    )(hidden, down)


def grad_down_kernel(hidden_ref, rows_ref, gate_ref, out_ref, scaled_ref):
    @pl.when(pl.program_id(0) == 0)
    def _():
        scaled_ref[...] = (gate_ref[...] * rows_ref[...].astype(f32)).astype(bf16)

    out_ref[0] = lax.dot_general(
        hidden_ref[0], scaled_ref[...], (((0,), (0,)), ((), ())), preferred_element_type=f32
    ).astype(bf16)


def grad_down_of(hidden, rows, gate):
    parts, count, share = hidden.shape
    width = rows.shape[1]
    return pl.pallas_call(
        grad_down_kernel,
        grid=(parts,),
        in_specs=[
            pl.BlockSpec((1, count, share), lambda g: (g, 0, 0)),
            pl.BlockSpec((count, width), lambda g: (0, 0)),
            pl.BlockSpec((count, 1), lambda g: (0, 0)),
        ],
        out_specs=pl.BlockSpec((1, share, width), lambda g: (0, g, 0)),
        out_shape=jax.ShapeDtypeStruct((1, parts * share, width), bf16),
        scratch_shapes=[pltpu.VMEM((count, width), bf16)],
        compiler_params=pltpu.CompilerParams(vmem_limit_bytes=VMEM_LIMIT),
        cost_estimate=pl.CostEstimate(
            flops=2 * count * width * parts * share, bytes_accessed=12_500_000, transcendentals=0
        ),
    )(hidden, rows, gate)


def exchange(value, axes):
    return lax.all_to_all(value, axes, split_axis=0, concat_axis=0, tiled=True)


def spread(value, axes, copies):
    return exchange(jnp.broadcast_to(value[None], (copies,) + value.shape), axes)


def swap(pieces, axes, size, stride=1):
    got = [pieces[0]]
    for k in range(1, size // stride):
        pairs = [(i, (i + k * stride) % size) for i in range(size)]
        got.append(lax.ppermute(pieces[k], axes, pairs))
    return got


def to_neighbour(value):
    return lax.ppermute(value, "z", [(i, i ^ 1) for i in range(8)])


def total_of(pieces):
    total = pieces[0].astype(f32)
    for piece in pieces[1:]:
        total = total + piece.astype(f32)
    return total


BLOCK = 40
PADDED = 8 * BLOCK
SHARE = LATENT // 8


def block_of(piece, z_at, sign):
    base = z_at + sign * 2 * (piece // 2)
    base = jnp.where(base >= 8, base - 8, jnp.where(base < 0, base + 8, base))
    other = jnp.where(base % 2 == 0, base + 1, base - 1)
    return jnp.where(piece % 2 == 0, base, other)


def cut_kernel(z_ref, total_ref, *refs):
    outs = refs[2:]
    row = lax.broadcasted_iota(jnp.int32, (PADDED, LATENT), 0)
    column = lax.broadcasted_iota(jnp.int32, (PADDED, LATENT), 1)
    piece = row // BLOCK
    within = row - piece * BLOCK
    block = block_of(piece, z_ref[0], 1)
    source = jnp.where(within < SHARE, block * SHARE + within, -1)
    pick = jnp.where(source == column, 1.0, 0.0).astype(bf16)
    rows = jnp.dot(pick, total_ref[...], preferred_element_type=f32)
    for k in range(4):
        outs[k][...] = rows[2 * k * BLOCK : 2 * (k + 1) * BLOCK].astype(bf16)


def gram_kernel(z_ref, *refs):
    parts, whole_ref, gram_ref = refs[:4], refs[4], refs[5]
    rows = jnp.concatenate([part[...].astype(f32) for part in parts], axis=0).astype(bf16)
    row = lax.broadcasted_iota(jnp.int32, (LATENT, PADDED), 0)
    column = lax.broadcasted_iota(jnp.int32, (LATENT, PADDED), 1)
    piece = column // BLOCK
    within = column - piece * BLOCK
    block = block_of(piece, z_ref[0], -1)
    target = jnp.where(within < SHARE, block * SHARE + within, -1)
    pick = jnp.where(target == row, 1.0, 0.0).astype(bf16)
    whole = jnp.dot(pick, rows, preferred_element_type=f32).astype(bf16)
    whole_ref[...] = whole
    gram_ref[...] = lax.dot_general(
        whole, whole, (((1,), (1,)), ((), ())), preferred_element_type=f32
    )


def newton_kernel(grams_ref, whole_ref, after_ref, out_ref):
    gram = total_of([grams_ref[g] for g in range(grams_ref.shape[0])])
    row = lax.broadcasted_iota(jnp.int32, (LATENT, LATENT), 0)
    column = lax.broadcasted_iota(jnp.int32, (LATENT, LATENT), 1)
    eye = jnp.where(row == column, 1.0, 0.0)
    squares = jnp.sum(jnp.sum(gram * eye, axis=1, keepdims=True), axis=0, keepdims=True)
    inverse = 1.0 / (jnp.sqrt(squares) + NORM_EPS)
    dot = lambda a, b: jnp.dot(
        a, b, precision=lax.Precision.HIGHEST, preferred_element_type=f32
    )
    first = gram * inverse * inverse
    poly_first = COEF_A * eye + COEF_B * first + COEF_C * dot(first, first)
    second = dot(poly_first, dot(first, poly_first))
    poly_second = COEF_A * eye + COEF_B * second + COEF_C * dot(second, second)
    factor = 0.2 * float(D) ** 0.5
    both = dot(poly_second, poly_first) * (factor * inverse)
    high = both.astype(bf16)
    low = (both - high.astype(f32)).astype(bf16)
    whole = whole_ref[...]
    out_ref[...] = (
        jnp.dot(high, whole, preferred_element_type=f32)
        + jnp.dot(low, whole, preferred_element_type=f32)
    ).astype(bf16)


SMEM = pl.BlockSpec(memory_space=pltpu.SMEM)
WHOLE = pl.BlockSpec(memory_space=pltpu.VMEM)


PAIR = jax.ShapeDtypeStruct((2 * BLOCK, D // 8), bf16)
AFTER = pl.BlockSpec(memory_space=pl.ANY)
PARAMS = pltpu.CompilerParams(vmem_limit_bytes=VMEM_LIMIT)


def muon_blocks(attention, *after):
    part = lax.psum_scatter(attention, "y", scatter_dimension=0, tiled=True)[0]
    return pl.pallas_call(
        cut_kernel,
        in_specs=[SMEM, WHOLE, AFTER, AFTER],
        out_specs=[WHOLE] * 4,
        out_shape=[PAIR] * 4,
        compiler_params=PARAMS,
        cost_estimate=pl.CostEstimate(flops=170_000_000, bytes_accessed=1_200_000, transcendentals=0),
    )(lax.axis_index("z")[None], part, *after)


def muon_gram(row_block):
    pair = jnp.concatenate([row_block, to_neighbour(row_block)], axis=0)
    gathered = swap([pair] * 4, "z", 8, 2)
    return pl.pallas_call(
        gram_kernel,
        in_specs=[SMEM] + [WHOLE] * 4,
        out_specs=[WHOLE] * 2,
        out_shape=[
            jax.ShapeDtypeStruct((LATENT, D // 8), bf16),
            jax.ShapeDtypeStruct((LATENT, LATENT), f32),
        ],
        compiler_params=PARAMS,
        cost_estimate=pl.CostEstimate(flops=300_000_000, bytes_accessed=1_600_000, transcendentals=0),
    )(lax.axis_index("z")[None], *gathered)


def muon_update_of(whole, grams, after):
    return pl.pallas_call(
        newton_kernel,
        in_specs=[WHOLE, WHOLE, AFTER],
        out_specs=WHOLE,
        out_shape=jax.ShapeDtypeStruct((LATENT, D // 8), bf16),
        compiler_params=PARAMS,
        cost_estimate=pl.CostEstimate(
            flops=3_000_000_000, bytes_accessed=3_600_000, transcendentals=0
        ),
    )(grams, whole, after)


def muon_spread(update):
    y_at = lax.axis_index("y")
    out = jnp.zeros((4,) + update.shape, bf16)
    for k, got in enumerate(swap([update] * 4, "y", 4)):
        out = lax.dynamic_update_index_in_dim(out, got, lax.rem(y_at + 4 - k, 4), 0)
    return out


def join_kernel(first_ref, second_ref, after_ref, out_ref):
    out_ref[:, 0, :] = first_ref[...]
    out_ref[:, 1, :] = second_ref[...]


def join(first, second, after):
    return pl.pallas_call(
        join_kernel,
        in_specs=[WHOLE, WHOLE, AFTER],
        out_specs=WHOLE,
        out_shape=jax.ShapeDtypeStruct((first.shape[0], 2, first.shape[1]), f32),
        compiler_params=PARAMS,
    )(first, second, after)


def hand_kernel(value_ref, *refs):
    refs[-1][...] = value_ref[...]


def hand(value, *after):
    return pl.pallas_call(
        hand_kernel,
        in_specs=[WHOLE] + [AFTER] * len(after),
        out_specs=WHOLE,
        out_shape=jax.ShapeDtypeStruct(value.shape, value.dtype),
        compiler_params=PARAMS,
    )(value, *after)


def add_kernel(values_ref, *refs):
    total = values_ref[0]
    for i in range(1, values_ref.shape[0]):
        total = total + values_ref[i]
    refs[-1][...] = total


def add_up(values, *after):
    return pl.pallas_call(
        add_kernel,
        in_specs=[WHOLE] + [AFTER] * len(after),
        out_specs=WHOLE,
        out_shape=jax.ShapeDtypeStruct(values.shape[1:], values.dtype),
        compiler_params=PARAMS,
    )(values, *after)


def on_device(
    out_grad,
    router_input,
    router_weight,
    routes,
    balance_grad,
    saved_hidden,
    expert_down,
    attention_grads,
):
    width = out_grad.shape[1]
    down = expert_down[0]
    share = saved_hidden.shape[3]
    count = CAP * EXPERTS
    weight_t = router_weight.T
    input_f = router_input.astype(f32)
    routes_t = routes.T
    routes_rows = jnp.pad(routes_t.astype(bf16), ((0, 8), (0, width - TOK)))
    tokens = jnp.concatenate([out_grad, routes_rows], axis=0)
    blocks_got = lax.all_gather(tokens, "z", axis=0, tiled=False)
    packed = pack(blocks_got, lax.axis_index("z"))
    rows_got = exchange(packed, "y")
    position, partial_logits = place(routes_t, router_input, weight_t)
    logits = total_of(swap([partial_logits] * 8, FS, 8))

    scores = jax.nn.sigmoid(logits)
    chosen = position >= 0.0
    selected = chosen.astype(f32)
    score_total = jnp.sum(selected * scores, axis=0, keepdims=True)
    gates = (selected * ROUTE_SCALE * scores / score_total).astype(bf16).astype(f32)
    slot_ids = jnp.arange(SLOTS, dtype=jnp.int32).astype(f32)
    matches = position[:, None, :] == slot_ids[None, :, None]
    slot_gates = jnp.sum(jnp.where(matches, gates[:, None, :], 0.0), axis=2)
    hidden_share = jnp.swapaxes(saved_hidden[0], 0, 1).reshape(count, share)
    hidden = lax.all_gather(hand(hidden_share, slot_gates), FS, axis=0, tiled=False)
    back = hidden_times_down(hidden, down)
    blocks = muon_blocks(attention_grads[0], slot_gates, packed)
    pair_sum = total_of(swap(blocks, "z", 8, 2))
    for_next = to_neighbour(pair_sum[BLOCK:].astype(bf16))
    row_block = (pair_sum[:BLOCK] + for_next.astype(f32)).astype(bf16)
    whole, gram = muon_gram(row_block)
    grams = lax.all_gather(gram, FS, axis=0, tiled=False)
    keep = jnp.where(back[0, 0] < f32(jnp.inf), 1.0, 0.0).astype(bf16)
    rows = jnp.transpose(rows_got[:, :, :CAP] * keep, (2, 1, 0, 3)).reshape(count, width)
    gate_part = jnp.sum(back * rows.astype(f32), axis=1)
    gate_part_t = jnp.pad(gate_part.reshape(CAP, EXPERTS).T, ((0, 0), (0, SLOTS - CAP)))
    joined = join(slot_gates, gate_part_t, position)
    both_got = exchange(joined, EP)
    gate_column = both_got[:, 0, :CAP].T.reshape(count, 1)
    returned = both_got[:, 1]
    back_part = jnp.sum(jnp.where(matches, returned[:, :, None], 0.0), axis=1)
    grad_down = grad_down_of(hidden, rows, gate_column)
    x_at, core_at = lax.axis_index("x"), lax.axis_index("c")
    for_other = upstream_partial(rows, down, x_at, 1 - core_at, joined)
    from_other = lax.ppermute(for_other, "c", [(0, 1), (1, 0)])
    for_own = upstream_partial(rows, down, x_at, core_at, for_other)
    both_cores = (from_other.astype(f32) + for_own.astype(f32)).astype(bf16)
    upstream = total_of(swap([both_cores[k] for k in range(4)], "x", 4))
    back_parts = spread(hand(back_part, for_own), FS, 8)
    gate_back = add_up(back_parts, grad_down, both_cores)

    grad_hidden = (gate_column * upstream).astype(bf16)
    grad_hidden = jnp.swapaxes(grad_hidden.reshape(CAP, EXPERTS, share), 0, 1)[None]

    weighted = jnp.sum(selected * gate_back * scores, axis=0, keepdims=True) / score_total
    score_grad = balance_grad.T + selected * (ROUTE_SCALE / score_total) * (gate_back - weighted)
    logit_grad = score_grad * scores * (1.0 - scores)
    router_part = jnp.dot(logit_grad, input_f, precision=lax.Precision.HIGHEST)
    router_got = exchange(router_part.reshape(EXPERTS, 1, width), EP)
    update = muon_update_of(whole, grams, router_part)
    muon_update = muon_spread(update)
    router_row = add_up(router_got, update, upstream)
    router_grad = spread(router_row, EP, EXPERTS).reshape(EXPERTS, width).T
    token_grad = lax.dot_general(
        logit_grad, weight_t, (((0,), (0,)), ((), ())), precision=lax.Precision.HIGHEST
    ).astype(bf16)
    return (grad_hidden, grad_down, router_grad, token_grad, muon_update)


def solution(mesh):
    split = Mesh(mesh.devices.reshape(4, 2, 8, 4), ("x", "c", "z", "y"))
    in_specs = (
        P(EP, FS),
        P(EP, FS),
        P(FS, None),
        P(EP, None),
        P(EP, None),
        P(EP, None, None, FS),
        P(EP, None, FS),
        P(EP, None, None, FS),
    )
    out_specs = (
        P(EP, None, None, FS),
        P(EP, None, FS),
        P(FS, None),
        P(EP, FS),
        P(None, None, FS),
    )
    return jax.shard_map(
        on_device, mesh=split, in_specs=in_specs, out_specs=out_specs, check_vma=False
    )
```

```python
import jax
import jax.numpy as jnp
from jax import lax
from jax.experimental import pallas as pl
from jax.experimental.pallas import tpu as pltpu
from jax.sharding import Mesh, PartitionSpec as P

D = 7168
LATENT = 288
ROUTE_SCALE = 2.827
NORM_EPS = 1e-07
COEF_A = 3.4445
COEF_B = -4.775
COEF_C = 2.0315
CAP = 36
SLOTS = 40
EXPERTS = 32
TOK = 128

FS = ("x", "c")
EP = ("z", "y")
f32 = jnp.float32
bf16 = jnp.bfloat16
VMEM_LIMIT = 48 * 1024 * 1024


def pack_kernel(routes_ref, tokens_ref, input_ref, weight_ref, out_ref, pos_ref, logit_ref):
    expert_ids = lax.broadcasted_iota(jnp.int32, (EXPERTS, TOK), 0)
    chosen = jnp.zeros((EXPERTS, TOK), f32)
    for k in range(routes_ref.shape[0]):
        chosen = chosen + jnp.where(routes_ref[k : k + 1, :] == expert_ids, 1.0, 0.0)
    before = lax.broadcasted_iota(jnp.int32, (TOK, TOK), 0)
    after = lax.broadcasted_iota(jnp.int32, (TOK, TOK), 1)
    upper = jnp.where(before <= after, 1.0, 0.0).astype(bf16)
    counted = jnp.dot(chosen.astype(bf16), upper, preferred_element_type=f32)
    position = jnp.where(chosen > 0.0, counted - 1.0, -1.0)
    pos_ref[...] = position
    slot_ids = lax.broadcasted_iota(jnp.int32, (SLOTS, TOK), 0).astype(f32)
    tokens = tokens_ref[...]
    group = 8
    for start in range(0, EXPERTS, group):
        picks = [
            jnp.where(slot_ids == position[e : e + 1, :], 1.0, 0.0)
            for e in range(start, start + group)
        ]
        pick = jnp.concatenate(picks, axis=0).astype(bf16)
        rows = jnp.dot(pick, tokens, preferred_element_type=f32)
        for i in range(group):
            out_ref[start + i] = rows[i * SLOTS : (i + 1) * SLOTS].astype(bf16)
    rest = weight_ref[...]
    logits = jnp.zeros((EXPERTS, TOK), f32)
    for _ in range(3):
        term = rest.astype(bf16)
        rest = rest - term.astype(f32)
        logits = logits + lax.dot_general(
            term, input_ref[...], (((1,), (1,)), ((), ())), preferred_element_type=f32
        )
    logit_ref[...] = logits


def pack(routes_t, tokens, router_input, weight_t):
    width = tokens.shape[1]
    return pl.pallas_call(
        pack_kernel,
        out_shape=(
            jax.ShapeDtypeStruct((EXPERTS, SLOTS, width), bf16),
            jax.ShapeDtypeStruct((EXPERTS, TOK), f32),
            jax.ShapeDtypeStruct((EXPERTS, TOK), f32),
        ),
        compiler_params=pltpu.CompilerParams(vmem_limit_bytes=VMEM_LIMIT),
        cost_estimate=pl.CostEstimate(flops=300_000_000, bytes_accessed=2_800_000, transcendentals=0),
    )(routes_t, tokens, router_input, weight_t)


def upstream_kernel(first_ref, rows_ref, down_ref, *refs):
    refs[-1][0] = lax.dot_general(
        rows_ref[...], down_ref[...], (((1,), (1,)), ((), ())), preferred_element_type=f32
    ).astype(bf16)


def upstream_partial(rows, down, place, core, after):
    count, width = rows.shape
    share = down.shape[0] // 8
    grid_spec = pltpu.PrefetchScalarGridSpec(
        num_scalar_prefetch=1,
        grid=(4,),
        in_specs=[
            pl.BlockSpec((count, width), lambda g, p: (0, 0)),
            pl.BlockSpec((share, width), lambda g, p: (2 * lax.rem(p[0] + g, 4) + p[1], 0)),
            pl.BlockSpec(memory_space=pl.ANY),
        ],
        out_specs=pl.BlockSpec((1, count, share), lambda g, p: (g, 0, 0)),
    )
    return pl.pallas_call(
        upstream_kernel,
        grid_spec=grid_spec,
        out_shape=jax.ShapeDtypeStruct((4, count, share), bf16),
        compiler_params=pltpu.CompilerParams(vmem_limit_bytes=VMEM_LIMIT),
        cost_estimate=pl.CostEstimate(
            flops=count * width * down.shape[0], bytes_accessed=6_300_000, transcendentals=0
        ),
    )(jnp.stack([place, core]), rows, down, after)


def back_kernel(hidden_ref, down_ref, out_ref):
    parts = hidden_ref.shape[0]
    whole = jnp.concatenate([hidden_ref[g] for g in range(parts)], axis=1)
    out_ref[...] = jnp.dot(whole, down_ref[...], preferred_element_type=f32)


def hidden_times_down(hidden, down):
    parts, count, share = hidden.shape
    width = down.shape[1]
    steps = 4
    block = count // steps
    return pl.pallas_call(
        back_kernel,
        grid=(steps,),
        in_specs=[
            pl.BlockSpec((parts, block, share), lambda g: (0, g, 0)),
            pl.BlockSpec((parts * share, width), lambda g: (0, 0)),
        ],
        out_specs=pl.BlockSpec((block, width), lambda g: (g, 0)),
        out_shape=jax.ShapeDtypeStruct((count, width), f32),
        compiler_params=pltpu.CompilerParams(vmem_limit_bytes=VMEM_LIMIT),
        cost_estimate=pl.CostEstimate(
            flops=2 * count * width * down.shape[0], bytes_accessed=12_500_000, transcendentals=0
        ),
    )(hidden, down)


def grad_down_kernel(hidden_ref, rows_ref, gate_ref, out_ref, scaled_ref):
    @pl.when(pl.program_id(0) == 0)
    def _():
        scaled_ref[...] = (gate_ref[...] * rows_ref[...].astype(f32)).astype(bf16)

    out_ref[0] = lax.dot_general(
        hidden_ref[0], scaled_ref[...], (((0,), (0,)), ((), ())), preferred_element_type=f32
    ).astype(bf16)


def grad_down_of(hidden, rows, gate):
    parts, count, share = hidden.shape
    width = rows.shape[1]
    return pl.pallas_call(
        grad_down_kernel,
        grid=(parts,),
        in_specs=[
            pl.BlockSpec((1, count, share), lambda g: (g, 0, 0)),
            pl.BlockSpec((count, width), lambda g: (0, 0)),
            pl.BlockSpec((count, 1), lambda g: (0, 0)),
        ],
        out_specs=pl.BlockSpec((1, share, width), lambda g: (0, g, 0)),
        out_shape=jax.ShapeDtypeStruct((1, parts * share, width), bf16),
        scratch_shapes=[pltpu.VMEM((count, width), bf16)],
        compiler_params=pltpu.CompilerParams(vmem_limit_bytes=VMEM_LIMIT),
        cost_estimate=pl.CostEstimate(
            flops=2 * count * width * parts * share, bytes_accessed=12_500_000, transcendentals=0
        ),
    )(hidden, rows, gate)


def exchange(value, axes):
    return lax.all_to_all(value, axes, split_axis=0, concat_axis=0, tiled=True)


def spread(value, axes, copies):
    return exchange(jnp.broadcast_to(value[None], (copies,) + value.shape), axes)


def swap(pieces, axes, size, stride=1):
    got = [pieces[0]]
    for k in range(1, size // stride):
        pairs = [(i, (i + k * stride) % size) for i in range(size)]
        got.append(lax.ppermute(pieces[k], axes, pairs))
    return got


def to_neighbour(value):
    return lax.ppermute(value, "z", [(i, i ^ 1) for i in range(8)])


def total_of(pieces):
    total = pieces[0].astype(f32)
    for piece in pieces[1:]:
        total = total + piece.astype(f32)
    return total


BLOCK = 40
PADDED = 8 * BLOCK
SHARE = LATENT // 8


def block_of(piece, z_at, sign):
    base = z_at + sign * 2 * (piece // 2)
    base = jnp.where(base >= 8, base - 8, jnp.where(base < 0, base + 8, base))
    other = jnp.where(base % 2 == 0, base + 1, base - 1)
    return jnp.where(piece % 2 == 0, base, other)


def cut_kernel(z_ref, total_ref, after_ref, *outs):
    row = lax.broadcasted_iota(jnp.int32, (PADDED, LATENT), 0)
    column = lax.broadcasted_iota(jnp.int32, (PADDED, LATENT), 1)
    piece = row // BLOCK
    within = row - piece * BLOCK
    block = block_of(piece, z_ref[0], 1)
    source = jnp.where(within < SHARE, block * SHARE + within, -1)
    pick = jnp.where(source == column, 1.0, 0.0).astype(bf16)
    rows = jnp.dot(pick, total_ref[...], preferred_element_type=f32)
    for k in range(4):
        outs[k][...] = rows[2 * k * BLOCK : 2 * (k + 1) * BLOCK].astype(bf16)


def pair_kernel(*refs):
    total = total_of([part[...] for part in refs[:4]])
    refs[5][...] = total[:BLOCK]
    refs[6][...] = total[BLOCK:].astype(bf16)


def gram_kernel(z_ref, *refs):
    parts, whole_ref, gram_ref = refs[:4], refs[5], refs[6]
    rows = jnp.concatenate([part[...].astype(f32) for part in parts], axis=0).astype(bf16)
    row = lax.broadcasted_iota(jnp.int32, (LATENT, PADDED), 0)
    column = lax.broadcasted_iota(jnp.int32, (LATENT, PADDED), 1)
    piece = column // BLOCK
    within = column - piece * BLOCK
    block = block_of(piece, z_ref[0], -1)
    target = jnp.where(within < SHARE, block * SHARE + within, -1)
    pick = jnp.where(target == row, 1.0, 0.0).astype(bf16)
    whole = jnp.dot(pick, rows, preferred_element_type=f32).astype(bf16)
    whole_ref[...] = whole
    gram_ref[...] = lax.dot_general(
        whole, whole, (((1,), (1,)), ((), ())), preferred_element_type=f32
    ).astype(bf16)


def newton_kernel(grams_ref, whole_ref, after_ref, out_ref):
    gram = total_of([grams_ref[g] for g in range(grams_ref.shape[0])])
    row = lax.broadcasted_iota(jnp.int32, (LATENT, LATENT), 0)
    column = lax.broadcasted_iota(jnp.int32, (LATENT, LATENT), 1)
    eye = jnp.where(row == column, 1.0, 0.0)
    squares = jnp.sum(jnp.sum(gram * eye, axis=1, keepdims=True), axis=0, keepdims=True)
    inverse = 1.0 / (jnp.sqrt(squares) + NORM_EPS)
    dot = lambda a, b: jnp.dot(
        a, b, precision=lax.Precision.HIGHEST, preferred_element_type=f32
    )
    first = gram * inverse * inverse
    poly_first = COEF_A * eye + COEF_B * first + COEF_C * dot(first, first)
    second = dot(poly_first, dot(first, poly_first))
    poly_second = COEF_A * eye + COEF_B * second + COEF_C * dot(second, second)
    factor = 0.2 * float(D) ** 0.5
    both = dot(poly_second, poly_first) * (factor * inverse)
    high = both.astype(bf16)
    low = (both - high.astype(f32)).astype(bf16)
    whole = whole_ref[...]
    out_ref[...] = (
        jnp.dot(high, whole, preferred_element_type=f32)
        + jnp.dot(low, whole, preferred_element_type=f32)
    ).astype(bf16)


SMEM = pl.BlockSpec(memory_space=pltpu.SMEM)
WHOLE = pl.BlockSpec(memory_space=pltpu.VMEM)


PAIR = jax.ShapeDtypeStruct((2 * BLOCK, D // 8), bf16)
AFTER = pl.BlockSpec(memory_space=pl.ANY)
PARAMS = pltpu.CompilerParams(vmem_limit_bytes=VMEM_LIMIT)


def muon_blocks(attention, after):
    part = lax.psum_scatter(attention, "y", scatter_dimension=0, tiled=True)[0]
    return pl.pallas_call(
        cut_kernel,
        in_specs=[SMEM, WHOLE, AFTER],
        out_specs=[WHOLE] * 4,
        out_shape=[PAIR] * 4,
        compiler_params=PARAMS,
        cost_estimate=pl.CostEstimate(flops=170_000_000, bytes_accessed=1_200_000, transcendentals=0),
    )(lax.axis_index("z")[None], part, after)


def pair_sums(parts, after):
    width = parts[0].shape[1]
    return pl.pallas_call(
        pair_kernel,
        in_specs=[WHOLE] * 4 + [AFTER],
        out_specs=[WHOLE] * 2,
        out_shape=[
            jax.ShapeDtypeStruct((BLOCK, width), f32),
            jax.ShapeDtypeStruct((BLOCK, width), bf16),
        ],
        compiler_params=PARAMS,
    )(*parts, after)


def muon_gram(row_block, after):
    pair = jnp.concatenate([row_block, to_neighbour(row_block)], axis=0)
    gathered = swap([pair] * 4, "z", 8, 2)
    return pl.pallas_call(
        gram_kernel,
        in_specs=[SMEM] + [WHOLE] * 4 + [AFTER],
        out_specs=[WHOLE] * 2,
        out_shape=[
            jax.ShapeDtypeStruct((LATENT, D // 8), bf16),
            jax.ShapeDtypeStruct((LATENT, LATENT), bf16),
        ],
        compiler_params=PARAMS,
        cost_estimate=pl.CostEstimate(flops=300_000_000, bytes_accessed=1_600_000, transcendentals=0),
    )(lax.axis_index("z")[None], *gathered, after)


def muon_update_of(whole, grams, after):
    return pl.pallas_call(
        newton_kernel,
        in_specs=[WHOLE, WHOLE, AFTER],
        out_specs=WHOLE,
        out_shape=jax.ShapeDtypeStruct((LATENT, D // 8), bf16),
        compiler_params=PARAMS,
        cost_estimate=pl.CostEstimate(
            flops=3_000_000_000, bytes_accessed=3_600_000, transcendentals=0
        ),
    )(grams, whole, after)


def muon_spread(update):
    y_at = lax.axis_index("y")
    out = jnp.zeros((4,) + update.shape, bf16)
    for k, got in enumerate(swap([update] * 4, "y", 4)):
        out = lax.dynamic_update_index_in_dim(out, got, lax.rem(y_at + 4 - k, 4), 0)
    return out


def join_kernel(first_ref, second_ref, after_ref, out_ref):
    out_ref[:, 0, :] = first_ref[...]
    out_ref[:, 1, :] = second_ref[...]


def join(first, second, after):
    return pl.pallas_call(
        join_kernel,
        in_specs=[WHOLE, WHOLE, AFTER],
        out_specs=WHOLE,
        out_shape=jax.ShapeDtypeStruct((first.shape[0], 2, first.shape[1]), f32),
        compiler_params=PARAMS,
    )(first, second, after)


def hand_kernel(value_ref, *refs):
    refs[-1][...] = value_ref[...]


def hand(value, *after):
    return pl.pallas_call(
        hand_kernel,
        in_specs=[WHOLE] + [AFTER] * len(after),
        out_specs=WHOLE,
        out_shape=jax.ShapeDtypeStruct(value.shape, value.dtype),
        compiler_params=PARAMS,
    )(value, *after)


def add_kernel(values_ref, *refs):
    total = values_ref[0]
    for i in range(1, values_ref.shape[0]):
        total = total + values_ref[i]
    refs[-1][...] = total


def add_up(values, *after):
    return pl.pallas_call(
        add_kernel,
        in_specs=[WHOLE] + [AFTER] * len(after),
        out_specs=WHOLE,
        out_shape=jax.ShapeDtypeStruct(values.shape[1:], values.dtype),
        compiler_params=PARAMS,
    )(values, *after)


def on_device(
    out_grad,
    router_input,
    router_weight,
    routes,
    balance_grad,
    saved_hidden,
    expert_down,
    attention_grads,
):
    width = out_grad.shape[1]
    down = expert_down[0]
    share = saved_hidden.shape[3]
    count = CAP * EXPERTS
    weight_t = router_weight.T
    input_f = router_input.astype(f32)
    packed, position, partial_logits = pack(routes.T, out_grad, router_input, weight_t)
    rows_got = exchange(packed, EP)
    hidden_share = jnp.swapaxes(saved_hidden[0], 0, 1).reshape(count, share)
    hidden = lax.all_gather(hidden_share, FS, axis=0, tiled=False)
    logits = total_of(swap([partial_logits] * 8, FS, 8))

    scores = jax.nn.sigmoid(logits)
    chosen = position >= 0.0
    selected = chosen.astype(f32)
    score_total = jnp.sum(selected * scores, axis=0, keepdims=True)
    gates = (selected * ROUTE_SCALE * scores / score_total).astype(bf16).astype(f32)
    slot_ids = jnp.arange(SLOTS, dtype=jnp.int32).astype(f32)
    matches = position[:, None, :] == slot_ids[None, :, None]
    slot_gates = jnp.sum(jnp.where(matches, gates[:, None, :], 0.0), axis=2)
    back = hidden_times_down(hidden, down)
    blocks = muon_blocks(attention_grads[0], slot_gates)
    own_sum, next_sum = pair_sums(swap(blocks, "z", 8, 2), back)
    row_block = (own_sum + to_neighbour(next_sum).astype(f32)).astype(bf16)
    ready = (blocks[0][0, 0] < f32(jnp.inf)) & (back[0, 0] < f32(jnp.inf))
    keep = jnp.where(ready, 1.0, 0.0).astype(bf16)
    rows = jnp.swapaxes(rows_got[:, :CAP] * keep, 0, 1).reshape(count, width)
    gate_part = jnp.sum(back * rows.astype(f32), axis=1)
    gate_part_t = jnp.pad(gate_part.reshape(CAP, EXPERTS).T, ((0, 0), (0, SLOTS - CAP)))
    joined = join(slot_gates, gate_part_t, position)
    both_got = exchange(joined, EP)
    gate_column = both_got[:, 0, :CAP].T.reshape(count, 1)
    returned = both_got[:, 1]
    back_part = jnp.sum(jnp.where(matches, returned[:, :, None], 0.0), axis=1)
    grad_down = grad_down_of(hidden, rows, gate_column)
    x_at, core_at = lax.axis_index("x"), lax.axis_index("c")
    for_other = upstream_partial(rows, down, x_at, 1 - core_at, joined)
    from_other = lax.ppermute(for_other, "c", [(0, 1), (1, 0)])
    for_own = upstream_partial(rows, down, x_at, core_at, for_other)
    whole, gram = muon_gram(row_block, joined)
    grams = lax.all_gather(gram, FS, axis=0, tiled=False)
    both_cores = (from_other.astype(f32) + for_own.astype(f32)).astype(bf16)
    upstream = total_of(swap([both_cores[k] for k in range(4)], "x", 4))
    back_parts = spread(hand(back_part, for_own), FS, 8)
    gate_back = add_up(back_parts, grad_down)

    grad_hidden = (gate_column * upstream).astype(bf16)
    grad_hidden = jnp.swapaxes(grad_hidden.reshape(CAP, EXPERTS, share), 0, 1)[None]

    weighted = jnp.sum(selected * gate_back * scores, axis=0, keepdims=True) / score_total
    score_grad = balance_grad.T + selected * (ROUTE_SCALE / score_total) * (gate_back - weighted)
    logit_grad = score_grad * scores * (1.0 - scores)
    router_part = jnp.dot(logit_grad, input_f, precision=lax.Precision.HIGHEST)
    router_got = exchange(router_part.reshape(EXPERTS, 1, width), EP)
    update = muon_update_of(whole, grams, router_part)
    muon_update = muon_spread(update)
    router_row = add_up(router_got, update)
    router_grad = spread(router_row, EP, EXPERTS).reshape(EXPERTS, width).T
    token_grad = lax.dot_general(
        logit_grad, weight_t, (((0,), (0,)), ((), ())), precision=lax.Precision.HIGHEST
    ).astype(bf16)
    return (grad_hidden, grad_down, router_grad, token_grad, muon_update)


def solution(mesh):
    split = Mesh(mesh.devices.reshape(4, 2, 8, 4), ("x", "c", "z", "y"))
    in_specs = (
        P(EP, FS),
        P(EP, FS),
        P(FS, None),
        P(EP, None),
        P(EP, None),
        P(EP, None, None, FS),
        P(EP, None, FS),
        P(EP, None, None, FS),
    )
    out_specs = (
        P(EP, None, None, FS),
        P(EP, None, FS),
        P(FS, None),
        P(EP, FS),
        P(None, None, FS),
    )
    return jax.shard_map(
        on_device, mesh=split, in_specs=in_specs, out_specs=out_specs, check_vma=False
    )
```

```python
import jax
import jax.numpy as jnp
from jax import lax
from jax.experimental import pallas as pl
from jax.experimental.pallas import tpu as pltpu
from jax.sharding import Mesh, PartitionSpec as P

D = 7168
LATENT = 288
ROUTE_SCALE = 2.827
NORM_EPS = 1e-07
COEF_A = 3.4445
COEF_B = -4.775
COEF_C = 2.0315
CAP = 36
SLOTS = 40
EXPERTS = 32
TOK = 128

FS = ("x", "c")
EP = ("z", "y")
f32 = jnp.float32
bf16 = jnp.bfloat16
VMEM_LIMIT = 48 * 1024 * 1024


def pack_kernel(routes_ref, tokens_ref, input_ref, weight_ref, out_ref, pos_ref, logit_ref):
    expert_ids = lax.broadcasted_iota(jnp.int32, (EXPERTS, TOK), 0)
    chosen = jnp.zeros((EXPERTS, TOK), f32)
    for k in range(routes_ref.shape[0]):
        chosen = chosen + jnp.where(routes_ref[k : k + 1, :] == expert_ids, 1.0, 0.0)
    before = lax.broadcasted_iota(jnp.int32, (TOK, TOK), 0)
    after = lax.broadcasted_iota(jnp.int32, (TOK, TOK), 1)
    upper = jnp.where(before <= after, 1.0, 0.0).astype(bf16)
    counted = jnp.dot(chosen.astype(bf16), upper, preferred_element_type=f32)
    position = jnp.where(chosen > 0.0, counted - 1.0, -1.0)
    pos_ref[...] = position
    slot_ids = lax.broadcasted_iota(jnp.int32, (SLOTS, TOK), 0).astype(f32)
    tokens = tokens_ref[...]
    group = 8
    for start in range(0, EXPERTS, group):
        picks = [
            jnp.where(slot_ids == position[e : e + 1, :], 1.0, 0.0)
            for e in range(start, start + group)
        ]
        pick = jnp.concatenate(picks, axis=0).astype(bf16)
        rows = jnp.dot(pick, tokens, preferred_element_type=f32)
        for i in range(group):
            out_ref[start + i] = rows[i * SLOTS : (i + 1) * SLOTS].astype(bf16)
    rest = weight_ref[...]
    logits = jnp.zeros((EXPERTS, TOK), f32)
    for _ in range(3):
        term = rest.astype(bf16)
        rest = rest - term.astype(f32)
        logits = logits + lax.dot_general(
            term, input_ref[...], (((1,), (1,)), ((), ())), preferred_element_type=f32
        )
    logit_ref[...] = logits


def pack(routes_t, tokens, router_input, weight_t):
    width = tokens.shape[1]
    return pl.pallas_call(
        pack_kernel,
        out_shape=(
            jax.ShapeDtypeStruct((EXPERTS, SLOTS, width), bf16),
            jax.ShapeDtypeStruct((EXPERTS, TOK), f32),
            jax.ShapeDtypeStruct((EXPERTS, TOK), f32),
        ),
        compiler_params=pltpu.CompilerParams(vmem_limit_bytes=VMEM_LIMIT),
        cost_estimate=pl.CostEstimate(flops=300_000_000, bytes_accessed=2_800_000, transcendentals=0),
    )(routes_t, tokens, router_input, weight_t)


def upstream_kernel(first_ref, rows_ref, down_ref, *refs):
    refs[-1][0] = lax.dot_general(
        rows_ref[...], down_ref[...], (((1,), (1,)), ((), ())), preferred_element_type=f32
    ).astype(bf16)


def upstream_partial(rows, down, place, core, after):
    count, width = rows.shape
    share = down.shape[0] // 8
    grid_spec = pltpu.PrefetchScalarGridSpec(
        num_scalar_prefetch=1,
        grid=(4,),
        in_specs=[
            pl.BlockSpec((count, width), lambda g, p: (0, 0)),
            pl.BlockSpec((share, width), lambda g, p: (2 * lax.rem(p[0] + g, 4) + p[1], 0)),
            pl.BlockSpec(memory_space=pl.ANY),
        ],
        out_specs=pl.BlockSpec((1, count, share), lambda g, p: (g, 0, 0)),
    )
    return pl.pallas_call(
        upstream_kernel,
        grid_spec=grid_spec,
        out_shape=jax.ShapeDtypeStruct((4, count, share), bf16),
        compiler_params=pltpu.CompilerParams(vmem_limit_bytes=VMEM_LIMIT),
        cost_estimate=pl.CostEstimate(
            flops=count * width * down.shape[0], bytes_accessed=6_300_000, transcendentals=0
        ),
    )(jnp.stack([place, core]), rows, down, after)


def back_kernel(hidden_ref, down_ref, out_ref):
    parts = hidden_ref.shape[0]
    whole = jnp.concatenate([hidden_ref[g] for g in range(parts)], axis=1)
    out_ref[...] = jnp.dot(whole, down_ref[...], preferred_element_type=f32)


def hidden_times_down(hidden, down):
    parts, count, share = hidden.shape
    width = down.shape[1]
    steps = 4
    block = count // steps
    return pl.pallas_call(
        back_kernel,
        grid=(steps,),
        in_specs=[
            pl.BlockSpec((parts, block, share), lambda g: (0, g, 0)),
            pl.BlockSpec((parts * share, width), lambda g: (0, 0)),
        ],
        out_specs=pl.BlockSpec((block, width), lambda g: (g, 0)),
        out_shape=jax.ShapeDtypeStruct((count, width), f32),
        compiler_params=pltpu.CompilerParams(vmem_limit_bytes=VMEM_LIMIT),
        cost_estimate=pl.CostEstimate(
            flops=2 * count * width * down.shape[0], bytes_accessed=12_500_000, transcendentals=0
        ),
    )(hidden, down)


def grad_down_kernel(hidden_ref, rows_ref, gate_ref, out_ref, scaled_ref):
    @pl.when(pl.program_id(0) == 0)
    def _():
        scaled_ref[...] = (gate_ref[...] * rows_ref[...].astype(f32)).astype(bf16)

    out_ref[0] = lax.dot_general(
        hidden_ref[0], scaled_ref[...], (((0,), (0,)), ((), ())), preferred_element_type=f32
    ).astype(bf16)


def grad_down_of(hidden, rows, gate):
    parts, count, share = hidden.shape
    width = rows.shape[1]
    return pl.pallas_call(
        grad_down_kernel,
        grid=(parts,),
        in_specs=[
            pl.BlockSpec((1, count, share), lambda g: (g, 0, 0)),
            pl.BlockSpec((count, width), lambda g: (0, 0)),
            pl.BlockSpec((count, 1), lambda g: (0, 0)),
        ],
        out_specs=pl.BlockSpec((1, share, width), lambda g: (0, g, 0)),
        out_shape=jax.ShapeDtypeStruct((1, parts * share, width), bf16),
        scratch_shapes=[pltpu.VMEM((count, width), bf16)],
        compiler_params=pltpu.CompilerParams(vmem_limit_bytes=VMEM_LIMIT),
        cost_estimate=pl.CostEstimate(
            flops=2 * count * width * parts * share, bytes_accessed=12_500_000, transcendentals=0
        ),
    )(hidden, rows, gate)


def exchange(value, axes):
    return lax.all_to_all(value, axes, split_axis=0, concat_axis=0, tiled=True)


def spread(value, axes, copies):
    return exchange(jnp.broadcast_to(value[None], (copies,) + value.shape), axes)


def swap(pieces, axes, size, stride=1):
    got = [pieces[0]]
    for k in range(1, size // stride):
        pairs = [(i, (i + k * stride) % size) for i in range(size)]
        got.append(lax.ppermute(pieces[k], axes, pairs))
    return got


def to_neighbour(value):
    return lax.ppermute(value, "z", [(i, i ^ 1) for i in range(8)])


def total_of(pieces):
    total = pieces[0].astype(f32)
    for piece in pieces[1:]:
        total = total + piece.astype(f32)
    return total


BLOCK = 40
PADDED = 8 * BLOCK
SHARE = LATENT // 8


def block_of(piece, z_at, sign):
    base = z_at + sign * 2 * (piece // 2)
    base = jnp.where(base >= 8, base - 8, jnp.where(base < 0, base + 8, base))
    other = jnp.where(base % 2 == 0, base + 1, base - 1)
    return jnp.where(piece % 2 == 0, base, other)


def cut_kernel(z_ref, total_ref, after_ref, *outs):
    row = lax.broadcasted_iota(jnp.int32, (PADDED, LATENT), 0)
    column = lax.broadcasted_iota(jnp.int32, (PADDED, LATENT), 1)
    piece = row // BLOCK
    within = row - piece * BLOCK
    block = block_of(piece, z_ref[0], 1)
    source = jnp.where(within < SHARE, block * SHARE + within, -1)
    pick = jnp.where(source == column, 1.0, 0.0).astype(bf16)
    rows = jnp.dot(pick, total_ref[...], preferred_element_type=f32)
    for k in range(4):
        outs[k][...] = rows[2 * k * BLOCK : 2 * (k + 1) * BLOCK].astype(bf16)


def pair_kernel(*refs):
    total = total_of([part[...] for part in refs[:4]])
    refs[5][...] = total[:BLOCK]
    refs[6][...] = total[BLOCK:].astype(bf16)


def gram_kernel(z_ref, *refs):
    parts, whole_ref, gram_ref = refs[:4], refs[5], refs[6]
    rows = jnp.concatenate([part[...].astype(f32) for part in parts], axis=0).astype(bf16)
    row = lax.broadcasted_iota(jnp.int32, (LATENT, PADDED), 0)
    column = lax.broadcasted_iota(jnp.int32, (LATENT, PADDED), 1)
    piece = column // BLOCK
    within = column - piece * BLOCK
    block = block_of(piece, z_ref[0], -1)
    target = jnp.where(within < SHARE, block * SHARE + within, -1)
    pick = jnp.where(target == row, 1.0, 0.0).astype(bf16)
    whole = jnp.dot(pick, rows, preferred_element_type=f32).astype(bf16)
    whole_ref[...] = whole
    gram_ref[...] = lax.dot_general(
        whole, whole, (((1,), (1,)), ((), ())), preferred_element_type=f32
    ).astype(bf16)


def newton_kernel(grams_ref, whole_ref, after_ref, out_ref):
    gram = total_of([grams_ref[g] for g in range(grams_ref.shape[0])])
    row = lax.broadcasted_iota(jnp.int32, (LATENT, LATENT), 0)
    column = lax.broadcasted_iota(jnp.int32, (LATENT, LATENT), 1)
    eye = jnp.where(row == column, 1.0, 0.0)
    squares = jnp.sum(jnp.sum(gram * eye, axis=1, keepdims=True), axis=0, keepdims=True)
    inverse = 1.0 / (jnp.sqrt(squares) + NORM_EPS)
    dot = lambda a, b: jnp.dot(
        a, b, precision=lax.Precision.HIGHEST, preferred_element_type=f32
    )
    first = gram * inverse * inverse
    poly_first = COEF_A * eye + COEF_B * first + COEF_C * dot(first, first)
    second = dot(poly_first, dot(first, poly_first))
    poly_second = COEF_A * eye + COEF_B * second + COEF_C * dot(second, second)
    factor = 0.2 * float(D) ** 0.5
    both = dot(poly_second, poly_first) * (factor * inverse)
    high = both.astype(bf16)
    low = (both - high.astype(f32)).astype(bf16)
    whole = whole_ref[...]
    out_ref[...] = (
        jnp.dot(high, whole, preferred_element_type=f32)
        + jnp.dot(low, whole, preferred_element_type=f32)
    ).astype(bf16)


SMEM = pl.BlockSpec(memory_space=pltpu.SMEM)
WHOLE = pl.BlockSpec(memory_space=pltpu.VMEM)


PAIR = jax.ShapeDtypeStruct((2 * BLOCK, D // 8), bf16)
AFTER = pl.BlockSpec(memory_space=pl.ANY)
PARAMS = pltpu.CompilerParams(vmem_limit_bytes=VMEM_LIMIT)


def muon_blocks(attention, after):
    part = lax.psum_scatter(attention, "y", scatter_dimension=0, tiled=True)[0]
    return pl.pallas_call(
        cut_kernel,
        in_specs=[SMEM, WHOLE, AFTER],
        out_specs=[WHOLE] * 4,
        out_shape=[PAIR] * 4,
        compiler_params=PARAMS,
        cost_estimate=pl.CostEstimate(flops=170_000_000, bytes_accessed=1_200_000, transcendentals=0),
    )(lax.axis_index("z")[None], part, after)


def pair_sums(parts, after):
    width = parts[0].shape[1]
    return pl.pallas_call(
        pair_kernel,
        in_specs=[WHOLE] * 4 + [AFTER],
        out_specs=[WHOLE] * 2,
        out_shape=[
            jax.ShapeDtypeStruct((BLOCK, width), f32),
            jax.ShapeDtypeStruct((BLOCK, width), bf16),
        ],
        compiler_params=PARAMS,
    )(*parts, after)


def muon_gram(row_block, after):
    pair = jnp.concatenate([row_block, to_neighbour(row_block)], axis=0)
    gathered = swap([pair] * 4, "z", 8, 2)
    return pl.pallas_call(
        gram_kernel,
        in_specs=[SMEM] + [WHOLE] * 4 + [AFTER],
        out_specs=[WHOLE] * 2,
        out_shape=[
            jax.ShapeDtypeStruct((LATENT, D // 8), bf16),
            jax.ShapeDtypeStruct((LATENT, LATENT), bf16),
        ],
        compiler_params=PARAMS,
        cost_estimate=pl.CostEstimate(flops=300_000_000, bytes_accessed=1_600_000, transcendentals=0),
    )(lax.axis_index("z")[None], *gathered, after)


def muon_update_of(whole, grams, after):
    return pl.pallas_call(
        newton_kernel,
        in_specs=[WHOLE, WHOLE, AFTER],
        out_specs=WHOLE,
        out_shape=jax.ShapeDtypeStruct((LATENT, D // 8), bf16),
        compiler_params=PARAMS,
        cost_estimate=pl.CostEstimate(
            flops=3_000_000_000, bytes_accessed=3_600_000, transcendentals=0
        ),
    )(grams, whole, after)


def join_kernel(first_ref, second_ref, after_ref, out_ref):
    out_ref[:, 0, :] = first_ref[...]
    out_ref[:, 1, :] = second_ref[...]


def join(first, second, after):
    return pl.pallas_call(
        join_kernel,
        in_specs=[WHOLE, WHOLE, AFTER],
        out_specs=WHOLE,
        out_shape=jax.ShapeDtypeStruct((first.shape[0], 2, first.shape[1]), f32),
        compiler_params=PARAMS,
    )(first, second, after)


def hand_kernel(value_ref, *refs):
    refs[-1][...] = value_ref[...]


def hand(value, *after):
    return pl.pallas_call(
        hand_kernel,
        in_specs=[WHOLE] + [AFTER] * len(after),
        out_specs=WHOLE,
        out_shape=jax.ShapeDtypeStruct(value.shape, value.dtype),
        compiler_params=PARAMS,
    )(value, *after)


def add_kernel(values_ref, *refs):
    total = values_ref[0]
    for i in range(1, values_ref.shape[0]):
        total = total + values_ref[i]
    refs[-1][...] = total


def add_up(values, *after):
    return pl.pallas_call(
        add_kernel,
        in_specs=[WHOLE] + [AFTER] * len(after),
        out_specs=WHOLE,
        out_shape=jax.ShapeDtypeStruct(values.shape[1:], values.dtype),
        compiler_params=PARAMS,
    )(values, *after)


def on_device(
    out_grad,
    router_input,
    router_weight,
    routes,
    balance_grad,
    saved_hidden,
    expert_down,
    attention_grads,
):
    width = out_grad.shape[1]
    down = expert_down[0]
    share = saved_hidden.shape[3]
    count = CAP * EXPERTS
    weight_t = router_weight.T
    input_f = router_input.astype(f32)
    packed, position, partial_logits = pack(routes.T, out_grad, router_input, weight_t)
    rows_got = exchange(packed, EP)
    hidden_share = jnp.swapaxes(saved_hidden[0], 0, 1).reshape(count, share)
    hidden = lax.all_gather(hidden_share, FS, axis=0, tiled=False)
    logits = total_of(swap([partial_logits] * 8, FS, 8))

    scores = jax.nn.sigmoid(logits)
    chosen = position >= 0.0
    selected = chosen.astype(f32)
    score_total = jnp.sum(selected * scores, axis=0, keepdims=True)
    gates = (selected * ROUTE_SCALE * scores / score_total).astype(bf16).astype(f32)
    slot_ids = jnp.arange(SLOTS, dtype=jnp.int32).astype(f32)
    matches = position[:, None, :] == slot_ids[None, :, None]
    slot_gates = jnp.sum(jnp.where(matches, gates[:, None, :], 0.0), axis=2)
    back = hidden_times_down(hidden, down)
    blocks = muon_blocks(attention_grads[0], slot_gates)
    own_sum, next_sum = pair_sums(swap(blocks, "z", 8, 2), back)
    row_block = (own_sum + to_neighbour(next_sum).astype(f32)).astype(bf16)
    ready = (blocks[0][0, 0] < f32(jnp.inf)) & (back[0, 0] < f32(jnp.inf))
    keep = jnp.where(ready, 1.0, 0.0).astype(bf16)
    rows = jnp.swapaxes(rows_got[:, :CAP] * keep, 0, 1).reshape(count, width)
    gate_part = jnp.sum(back * rows.astype(f32), axis=1)
    gate_part_t = jnp.pad(gate_part.reshape(CAP, EXPERTS).T, ((0, 0), (0, SLOTS - CAP)))
    joined = join(slot_gates, gate_part_t, position)
    both_got = exchange(joined, EP)
    gate_column = both_got[:, 0, :CAP].T.reshape(count, 1)
    returned = both_got[:, 1]
    back_part = jnp.sum(jnp.where(matches, returned[:, :, None], 0.0), axis=1)
    grad_down = grad_down_of(hidden, rows, gate_column)
    x_at, core_at = lax.axis_index("x"), lax.axis_index("c")
    for_other = upstream_partial(rows, down, x_at, 1 - core_at, joined)
    from_other = lax.ppermute(for_other, "c", [(0, 1), (1, 0)])
    for_own = upstream_partial(rows, down, x_at, core_at, for_other)
    whole, gram = muon_gram(row_block, joined)
    grams = lax.all_gather(gram, FS, axis=0, tiled=False)
    both_cores = (from_other.astype(f32) + for_own.astype(f32)).astype(bf16)
    upstream = total_of(swap([both_cores[k] for k in range(4)], "x", 4))
    back_parts = spread(hand(back_part, for_own), FS, 8)
    gate_back = add_up(back_parts, grad_down)

    grad_hidden = (gate_column * upstream).astype(bf16)
    grad_hidden = jnp.swapaxes(grad_hidden.reshape(CAP, EXPERTS, share), 0, 1)[None]

    weighted = jnp.sum(selected * gate_back * scores, axis=0, keepdims=True) / score_total
    score_grad = balance_grad.T + selected * (ROUTE_SCALE / score_total) * (gate_back - weighted)
    logit_grad = score_grad * scores * (1.0 - scores)
    router_part = jnp.dot(logit_grad, input_f, precision=lax.Precision.HIGHEST)
    router_got = exchange(router_part.reshape(EXPERTS, 1, width), EP)
    update = muon_update_of(whole, grams, router_part)
    muon_update = lax.all_gather(update, "y", axis=0, tiled=False)
    router_row = add_up(router_got, update)
    router_grad = spread(router_row, EP, EXPERTS).reshape(EXPERTS, width).T
    token_grad = lax.dot_general(
        logit_grad, weight_t, (((0,), (0,)), ((), ())), precision=lax.Precision.HIGHEST
    ).astype(bf16)
    return (grad_hidden, grad_down, router_grad, token_grad, muon_update)


def solution(mesh):
    split = Mesh(mesh.devices.reshape(4, 2, 8, 4), ("x", "c", "z", "y"))
    in_specs = (
        P(EP, FS),
        P(EP, FS),
        P(FS, None),
        P(EP, None),
        P(EP, None),
        P(EP, None, None, FS),
        P(EP, None, FS),
        P(EP, None, None, FS),
    )
    out_specs = (
        P(EP, None, None, FS),
        P(EP, None, FS),
        P(FS, None),
        P(EP, FS),
        P(None, None, FS),
    )
    return jax.shard_map(
        on_device, mesh=split, in_specs=in_specs, out_specs=out_specs, check_vma=False
    )
```

```python
import jax
import jax.numpy as jnp
from jax import lax
from jax.experimental import pallas as pl
from jax.experimental.pallas import tpu as pltpu
from jax.sharding import Mesh, PartitionSpec as P

D = 7168
LATENT = 288
ROUTE_SCALE = 2.827
NORM_EPS = 1e-07
COEF_A = 3.4445
COEF_B = -4.775
COEF_C = 2.0315
CAP = 36
SLOTS = 40
EXPERTS = 32
TOK = 128

FS = ("x", "c")
EP = ("z", "y")
f32 = jnp.float32
bf16 = jnp.bfloat16
VMEM_LIMIT = 48 * 1024 * 1024


def pack_kernel(routes_ref, tokens_ref, input_ref, weight_ref, out_ref, pos_ref, logit_ref):
    expert_ids = lax.broadcasted_iota(jnp.int32, (EXPERTS, TOK), 0)
    chosen = jnp.zeros((EXPERTS, TOK), f32)
    for k in range(routes_ref.shape[0]):
        chosen = chosen + jnp.where(routes_ref[k : k + 1, :] == expert_ids, 1.0, 0.0)
    before = lax.broadcasted_iota(jnp.int32, (TOK, TOK), 0)
    after = lax.broadcasted_iota(jnp.int32, (TOK, TOK), 1)
    upper = jnp.where(before <= after, 1.0, 0.0).astype(bf16)
    counted = jnp.dot(chosen.astype(bf16), upper, preferred_element_type=f32)
    position = jnp.where(chosen > 0.0, counted - 1.0, -1.0)
    pos_ref[...] = position
    slot_ids = lax.broadcasted_iota(jnp.int32, (SLOTS, TOK), 0).astype(f32)
    tokens = tokens_ref[...]
    group = 8
    for start in range(0, EXPERTS, group):
        picks = [
            jnp.where(slot_ids == position[e : e + 1, :], 1.0, 0.0)
            for e in range(start, start + group)
        ]
        pick = jnp.concatenate(picks, axis=0).astype(bf16)
        rows = jnp.dot(pick, tokens, preferred_element_type=f32)
        for i in range(group):
            out_ref[start + i] = rows[i * SLOTS : (i + 1) * SLOTS].astype(bf16)
    rest = weight_ref[...]
    logits = jnp.zeros((EXPERTS, TOK), f32)
    for _ in range(3):
        term = rest.astype(bf16)
        rest = rest - term.astype(f32)
        logits = logits + lax.dot_general(
            term, input_ref[...], (((1,), (1,)), ((), ())), preferred_element_type=f32
        )
    logit_ref[...] = logits


def pack(routes_t, tokens, router_input, weight_t):
    width = tokens.shape[1]
    return pl.pallas_call(
        pack_kernel,
        out_shape=(
            jax.ShapeDtypeStruct((EXPERTS, SLOTS, width), bf16),
            jax.ShapeDtypeStruct((EXPERTS, TOK), f32),
            jax.ShapeDtypeStruct((EXPERTS, TOK), f32),
        ),
        compiler_params=pltpu.CompilerParams(vmem_limit_bytes=VMEM_LIMIT),
        cost_estimate=pl.CostEstimate(flops=300_000_000, bytes_accessed=2_800_000, transcendentals=0),
    )(routes_t, tokens, router_input, weight_t)


def upstream_kernel(first_ref, rows_ref, down_ref, *refs):
    refs[-1][0] = lax.dot_general(
        rows_ref[...], down_ref[...], (((1,), (1,)), ((), ())), preferred_element_type=f32
    ).astype(bf16)


def upstream_partial(rows, down, place, core, after):
    count, width = rows.shape
    share = down.shape[0] // 8
    grid_spec = pltpu.PrefetchScalarGridSpec(
        num_scalar_prefetch=1,
        grid=(4,),
        in_specs=[
            pl.BlockSpec((count, width), lambda g, p: (0, 0)),
            pl.BlockSpec((share, width), lambda g, p: (2 * lax.rem(p[0] + g, 4) + p[1], 0)),
            pl.BlockSpec(memory_space=pl.ANY),
        ],
        out_specs=pl.BlockSpec((1, count, share), lambda g, p: (g, 0, 0)),
    )
    return pl.pallas_call(
        upstream_kernel,
        grid_spec=grid_spec,
        out_shape=jax.ShapeDtypeStruct((4, count, share), bf16),
        compiler_params=pltpu.CompilerParams(vmem_limit_bytes=VMEM_LIMIT),
        cost_estimate=pl.CostEstimate(
            flops=count * width * down.shape[0], bytes_accessed=6_300_000, transcendentals=0
        ),
    )(jnp.stack([place, core]), rows, down, after)


def back_kernel(hidden_ref, down_ref, out_ref):
    parts = hidden_ref.shape[0]
    whole = jnp.concatenate([hidden_ref[g] for g in range(parts)], axis=1)
    out_ref[...] = jnp.dot(whole, down_ref[...], preferred_element_type=f32)


def hidden_times_down(hidden, down):
    parts, count, share = hidden.shape
    width = down.shape[1]
    steps = 4
    block = count // steps
    return pl.pallas_call(
        back_kernel,
        grid=(steps,),
        in_specs=[
            pl.BlockSpec((parts, block, share), lambda g: (0, g, 0)),
            pl.BlockSpec((parts * share, width), lambda g: (0, 0)),
        ],
        out_specs=pl.BlockSpec((block, width), lambda g: (g, 0)),
        out_shape=jax.ShapeDtypeStruct((count, width), f32),
        compiler_params=pltpu.CompilerParams(vmem_limit_bytes=VMEM_LIMIT),
        cost_estimate=pl.CostEstimate(
            flops=2 * count * width * down.shape[0], bytes_accessed=12_500_000, transcendentals=0
        ),
    )(hidden, down)


def grad_down_kernel(hidden_ref, rows_ref, gate_ref, out_ref, scaled_ref):
    @pl.when(pl.program_id(0) == 0)
    def _():
        scaled_ref[...] = (gate_ref[...] * rows_ref[...].astype(f32)).astype(bf16)

    out_ref[0] = lax.dot_general(
        hidden_ref[0], scaled_ref[...], (((0,), (0,)), ((), ())), preferred_element_type=f32
    ).astype(bf16)


def grad_down_of(hidden, rows, gate):
    parts, count, share = hidden.shape
    width = rows.shape[1]
    return pl.pallas_call(
        grad_down_kernel,
        grid=(parts,),
        in_specs=[
            pl.BlockSpec((1, count, share), lambda g: (g, 0, 0)),
            pl.BlockSpec((count, width), lambda g: (0, 0)),
            pl.BlockSpec((count, 1), lambda g: (0, 0)),
        ],
        out_specs=pl.BlockSpec((1, share, width), lambda g: (0, g, 0)),
        out_shape=jax.ShapeDtypeStruct((1, parts * share, width), bf16),
        scratch_shapes=[pltpu.VMEM((count, width), bf16)],
        compiler_params=pltpu.CompilerParams(vmem_limit_bytes=VMEM_LIMIT),
        cost_estimate=pl.CostEstimate(
            flops=2 * count * width * parts * share, bytes_accessed=12_500_000, transcendentals=0
        ),
    )(hidden, rows, gate)


def exchange(value, axes):
    return lax.all_to_all(value, axes, split_axis=0, concat_axis=0, tiled=True)


def spread(value, axes, copies):
    return exchange(jnp.broadcast_to(value[None], (copies,) + value.shape), axes)


def swap(pieces, axes, size, stride=1):
    got = [pieces[0]]
    for k in range(1, size // stride):
        pairs = [(i, (i + k * stride) % size) for i in range(size)]
        got.append(lax.ppermute(pieces[k], axes, pairs))
    return got


def to_neighbour(value):
    return lax.ppermute(value, "z", [(i, i ^ 1) for i in range(8)])


def total_of(pieces):
    total = pieces[0].astype(f32)
    for piece in pieces[1:]:
        total = total + piece.astype(f32)
    return total


BLOCK = 40
PADDED = 8 * BLOCK
SHARE = LATENT // 8


def block_of(piece, z_at, sign):
    base = z_at + sign * 2 * (piece // 2)
    base = jnp.where(base >= 8, base - 8, jnp.where(base < 0, base + 8, base))
    other = jnp.where(base % 2 == 0, base + 1, base - 1)
    return jnp.where(piece % 2 == 0, base, other)


def cut_kernel(z_ref, total_ref, after_ref, *outs):
    row = lax.broadcasted_iota(jnp.int32, (PADDED, LATENT), 0)
    column = lax.broadcasted_iota(jnp.int32, (PADDED, LATENT), 1)
    piece = row // BLOCK
    within = row - piece * BLOCK
    block = block_of(piece, z_ref[0], 1)
    source = jnp.where(within < SHARE, block * SHARE + within, -1)
    pick = jnp.where(source == column, 1.0, 0.0).astype(bf16)
    rows = jnp.dot(pick, total_ref[...], preferred_element_type=f32)
    for k in range(4):
        outs[k][...] = rows[2 * k * BLOCK : 2 * (k + 1) * BLOCK].astype(bf16)


def pair_kernel(*refs):
    total = total_of([part[...] for part in refs[:4]])
    refs[5][...] = total[:BLOCK]
    refs[6][...] = total[BLOCK:].astype(bf16)


def gram_kernel(z_ref, *refs):
    parts, whole_ref, gram_ref = refs[:4], refs[5], refs[6]
    rows = jnp.concatenate([part[...].astype(f32) for part in parts], axis=0).astype(bf16)
    row = lax.broadcasted_iota(jnp.int32, (LATENT, PADDED), 0)
    column = lax.broadcasted_iota(jnp.int32, (LATENT, PADDED), 1)
    piece = column // BLOCK
    within = column - piece * BLOCK
    block = block_of(piece, z_ref[0], -1)
    target = jnp.where(within < SHARE, block * SHARE + within, -1)
    pick = jnp.where(target == row, 1.0, 0.0).astype(bf16)
    whole = jnp.dot(pick, rows, preferred_element_type=f32).astype(bf16)
    whole_ref[...] = whole
    gram_ref[...] = lax.dot_general(
        whole, whole, (((1,), (1,)), ((), ())), preferred_element_type=f32
    ).astype(bf16)


def newton_kernel(grams_ref, whole_ref, after_ref, out_ref):
    gram = total_of([grams_ref[g] for g in range(grams_ref.shape[0])])
    row = lax.broadcasted_iota(jnp.int32, (LATENT, LATENT), 0)
    column = lax.broadcasted_iota(jnp.int32, (LATENT, LATENT), 1)
    eye = jnp.where(row == column, 1.0, 0.0)
    squares = jnp.sum(jnp.sum(gram * eye, axis=1, keepdims=True), axis=0, keepdims=True)
    inverse = 1.0 / (jnp.sqrt(squares) + NORM_EPS)
    dot = lambda a, b: jnp.dot(
        a, b, precision=lax.Precision.HIGHEST, preferred_element_type=f32
    )
    first = gram * inverse * inverse
    poly_first = COEF_A * eye + COEF_B * first + COEF_C * dot(first, first)
    second = dot(poly_first, dot(first, poly_first))
    poly_second = COEF_A * eye + COEF_B * second + COEF_C * dot(second, second)
    factor = 0.2 * float(D) ** 0.5
    both = dot(poly_second, poly_first) * (factor * inverse)
    high = both.astype(bf16)
    low = (both - high.astype(f32)).astype(bf16)
    whole = whole_ref[...]
    out_ref[...] = (
        jnp.dot(high, whole, preferred_element_type=f32)
        + jnp.dot(low, whole, preferred_element_type=f32)
    ).astype(bf16)


SMEM = pl.BlockSpec(memory_space=pltpu.SMEM)
WHOLE = pl.BlockSpec(memory_space=pltpu.VMEM)


PAIR = jax.ShapeDtypeStruct((2 * BLOCK, D // 8), bf16)
AFTER = pl.BlockSpec(memory_space=pl.ANY)
PARAMS = pltpu.CompilerParams(vmem_limit_bytes=VMEM_LIMIT)


def muon_blocks(attention, after):
    part = lax.psum_scatter(attention, "y", scatter_dimension=0, tiled=True)[0]
    return pl.pallas_call(
        cut_kernel,
        in_specs=[SMEM, WHOLE, AFTER],
        out_specs=[WHOLE] * 4,
        out_shape=[PAIR] * 4,
        compiler_params=PARAMS,
        cost_estimate=pl.CostEstimate(flops=170_000_000, bytes_accessed=1_200_000, transcendentals=0),
    )(lax.axis_index("z")[None], part, after)


def pair_sums(parts, after):
    width = parts[0].shape[1]
    return pl.pallas_call(
        pair_kernel,
        in_specs=[WHOLE] * 4 + [AFTER],
        out_specs=[WHOLE] * 2,
        out_shape=[
            jax.ShapeDtypeStruct((BLOCK, width), f32),
            jax.ShapeDtypeStruct((BLOCK, width), bf16),
        ],
        compiler_params=PARAMS,
    )(*parts, after)


def muon_gram(row_block, after):
    pair = jnp.concatenate([row_block, to_neighbour(row_block)], axis=0)
    gathered = swap([pair] * 4, "z", 8, 2)
    return pl.pallas_call(
        gram_kernel,
        in_specs=[SMEM] + [WHOLE] * 4 + [AFTER],
        out_specs=[WHOLE] * 2,
        out_shape=[
            jax.ShapeDtypeStruct((LATENT, D // 8), bf16),
            jax.ShapeDtypeStruct((LATENT, LATENT), bf16),
        ],
        compiler_params=PARAMS,
        cost_estimate=pl.CostEstimate(flops=300_000_000, bytes_accessed=1_600_000, transcendentals=0),
    )(lax.axis_index("z")[None], *gathered, after)


def muon_update_of(whole, grams, after):
    return pl.pallas_call(
        newton_kernel,
        in_specs=[WHOLE, WHOLE, AFTER],
        out_specs=WHOLE,
        out_shape=jax.ShapeDtypeStruct((LATENT, D // 8), bf16),
        compiler_params=PARAMS,
        cost_estimate=pl.CostEstimate(
            flops=3_000_000_000, bytes_accessed=3_600_000, transcendentals=0
        ),
    )(grams, whole, after)


def join_kernel(first_ref, second_ref, after_ref, out_ref):
    out_ref[:, 0, :] = first_ref[...]
    out_ref[:, 1, :] = second_ref[...]


def join(first, second, after):
    return pl.pallas_call(
        join_kernel,
        in_specs=[WHOLE, WHOLE, AFTER],
        out_specs=WHOLE,
        out_shape=jax.ShapeDtypeStruct((first.shape[0], 2, first.shape[1]), f32),
        compiler_params=PARAMS,
    )(first, second, after)


def hand_kernel(value_ref, *refs):
    refs[-1][...] = value_ref[...]


def hand(value, *after):
    return pl.pallas_call(
        hand_kernel,
        in_specs=[WHOLE] + [AFTER] * len(after),
        out_specs=WHOLE,
        out_shape=jax.ShapeDtypeStruct(value.shape, value.dtype),
        compiler_params=PARAMS,
    )(value, *after)


def add_kernel(values_ref, *refs):
    total = values_ref[0]
    for i in range(1, values_ref.shape[0]):
        total = total + values_ref[i]
    refs[-1][...] = total


def add_up(values, *after):
    return pl.pallas_call(
        add_kernel,
        in_specs=[WHOLE] + [AFTER] * len(after),
        out_specs=WHOLE,
        out_shape=jax.ShapeDtypeStruct(values.shape[1:], values.dtype),
        compiler_params=PARAMS,
    )(values, *after)


def on_device(
    out_grad,
    router_input,
    router_weight,
    routes,
    balance_grad,
    saved_hidden,
    expert_down,
    attention_grads,
):
    width = out_grad.shape[1]
    down = expert_down[0]
    share = saved_hidden.shape[3]
    count = CAP * EXPERTS
    weight_t = router_weight.T
    input_f = router_input.astype(f32)
    packed, position, partial_logits = pack(routes.T, out_grad, router_input, weight_t)
    rows_got = exchange(packed, EP)
    hidden_share = jnp.swapaxes(saved_hidden[0], 0, 1).reshape(count, share)
    hidden = lax.all_gather(hidden_share, FS, axis=0, tiled=False)
    logits = total_of(swap([partial_logits] * 8, FS, 8))

    scores = jax.nn.sigmoid(logits)
    chosen = position >= 0.0
    selected = chosen.astype(f32)
    score_total = jnp.sum(selected * scores, axis=0, keepdims=True)
    gates = (selected * ROUTE_SCALE * scores / score_total).astype(bf16).astype(f32)
    slot_ids = jnp.arange(SLOTS, dtype=jnp.int32).astype(f32)
    matches = position[:, None, :] == slot_ids[None, :, None]
    slot_gates = jnp.sum(jnp.where(matches, gates[:, None, :], 0.0), axis=2)
    back = hidden_times_down(hidden, down)
    blocks = muon_blocks(attention_grads[0], slot_gates)
    own_sum, next_sum = pair_sums(swap(blocks, "z", 8, 2), back)
    row_block = (own_sum + to_neighbour(next_sum).astype(f32)).astype(bf16)
    ready = (blocks[0][0, 0] < f32(jnp.inf)) & (back[0, 0] < f32(jnp.inf))
    keep = jnp.where(ready, 1.0, 0.0).astype(bf16)
    rows = jnp.swapaxes(rows_got[:, :CAP] * keep, 0, 1).reshape(count, width)
    gate_part = jnp.sum(back * rows.astype(f32), axis=1)
    gate_part_t = jnp.pad(gate_part.reshape(CAP, EXPERTS).T, ((0, 0), (0, SLOTS - CAP)))
    joined = join(slot_gates, gate_part_t, position)
    both_got = exchange(joined, EP)
    gate_column = both_got[:, 0, :CAP].T.reshape(count, 1)
    returned = both_got[:, 1]
    back_part = jnp.sum(jnp.where(matches, returned[:, :, None], 0.0), axis=1)
    grad_down = grad_down_of(hidden, rows, gate_column)
    x_at, core_at = lax.axis_index("x"), lax.axis_index("c")
    for_other = upstream_partial(rows, down, x_at, 1 - core_at, joined)
    from_other = lax.ppermute(for_other, "c", [(0, 1), (1, 0)])
    for_own = upstream_partial(rows, down, x_at, core_at, for_other)
    whole, gram = muon_gram(row_block, joined)
    grams = lax.all_gather(gram, FS, axis=0, tiled=False)
    both_cores = (from_other.astype(f32) + for_own.astype(f32)).astype(bf16)
    upstream = total_of(swap([both_cores[k] for k in range(4)], "x", 4))
    back_parts = spread(hand(back_part, for_own), FS, 8)
    gate_back = add_up(back_parts, grad_down)

    grad_hidden = (gate_column * upstream).astype(bf16)
    grad_hidden = jnp.swapaxes(grad_hidden.reshape(CAP, EXPERTS, share), 0, 1)[None]

    weighted = jnp.sum(selected * gate_back * scores, axis=0, keepdims=True) / score_total
    score_grad = balance_grad.T + selected * (ROUTE_SCALE / score_total) * (gate_back - weighted)
    logit_grad = score_grad * scores * (1.0 - scores)
    router_part = jnp.dot(logit_grad, input_f, precision=lax.Precision.HIGHEST)
    router_got = exchange(router_part.reshape(EXPERTS, 1, width), EP)
    update = muon_update_of(whole, grams, for_own)
    muon_update = lax.all_gather(update, "y", axis=0, tiled=False)
    router_row = add_up(router_got, update)
    router_grad = spread(router_row, EP, EXPERTS).reshape(EXPERTS, width).T
    token_grad = lax.dot_general(
        logit_grad, weight_t, (((0,), (0,)), ((), ())), precision=lax.Precision.HIGHEST
    ).astype(bf16)
    return (grad_hidden, grad_down, router_grad, token_grad, muon_update)


def solution(mesh):
    split = Mesh(mesh.devices.reshape(4, 2, 8, 4), ("x", "c", "z", "y"))
    in_specs = (
        P(EP, FS),
        P(EP, FS),
        P(FS, None),
        P(EP, None),
        P(EP, None),
        P(EP, None, None, FS),
        P(EP, None, FS),
        P(EP, None, None, FS),
    )
    out_specs = (
        P(EP, None, None, FS),
        P(EP, None, FS),
        P(FS, None),
        P(EP, FS),
        P(None, None, FS),
    )
    return jax.shard_map(
        on_device, mesh=split, in_specs=in_specs, out_specs=out_specs, check_vma=False
    )
```
